512 devices in a mesh: dp: 32 (over y, z_lo), tp: 16 (over z_hi, x, core).
Axes of the slice: x: 4, y: 8, z: 8 (z_hi: 2, z_lo: 4; z = z_hi * 4 + z_lo), core: 2. Of those that a mesh axis runs over, the one named last changes fastest.
Arguments:
- activations: bfloat16 [64, 1024, 3584], P('dp', 'tp'), may hold values from -6 to 6
- out_grads: bfloat16 [64, 1024, 4096], P('dp', None, 'tp'), may hold values from -1.5 to 1.5
- clip_bound: float32 [1], replicated, may hold values from 3584 to 7168
Outputs:
- clipped_sum: float32 [3584, 4096], P('dp', 'tp')
The draws below stay inside these ranges and needn't reach their ends.
All inputs are finite; a program needn't handle non-finite values.
Results may differ from the reference program's by a relative error of at most 0.0003.
Values may be sent and summed in bfloat16 or wider, within the bound.
A program may use at most 64 MiB of HBM per device.

```python
import math
import jax
import jax.numpy as jnp
from jax import lax

D = 3584
QW = 4096
EX_DEV = 2
LEN_DEV = 64
LEN = 1024
EXAMPLES = 64
N_DP = 32
N_TP = 16


def feature_ramp(rise):
    position = jnp.arange(QW, dtype=jnp.float32) / jnp.float32(QW - 1)
    return jnp.exp(jnp.log(jnp.float32(rise)) * position).reshape(1, 1, QW)


def draw_out_grads(key, part):
    key = jax.random.fold_in(key, 7)
    key_scale, key_token, key_value = jax.random.split(key, 3)
    log_scale = jax.random.uniform(key_scale, (EX_DEV * N_DP, 1, 1), jnp.float32, jnp.log(2.5), jnp.log(8.0))
    values = jnp.clip(jax.random.normal(key_value, (EX_DEV * N_DP, LEN_DEV * N_TP, QW), jnp.float32), -6.0, 6.0)
    ramp = feature_ramp(2.0)
    token_scale = jax.random.uniform(key_token, (EX_DEV * N_DP, LEN_DEV * N_TP, 1), jnp.float32, 0.5, 2.0)
    length = jnp.float32(LEN_DEV * N_TP)
    result = values * jnp.exp(log_scale) * token_scale * ramp / jnp.sqrt(length)
    result = jnp.clip(result, -1.5, 1.5)
    return result.astype(jnp.bfloat16)


def shard_levels(stream_key, extent, shards, smallest, high):
    loudness = 1.0
    for axis_at, blocks in shards:
        steps = jax.random.uniform(jax.random.fold_in(jax.random.fold_in(stream_key, 6), axis_at), (blocks,), jnp.float32, smallest / len(shards), high / len(shards))
        loudness = loudness * jnp.repeat(jnp.exp(steps), extent[axis_at] // blocks).reshape((-1,) + (1,) * (len(extent) - 1 - axis_at))
    return loudness


def normal_values(rng, dims, width, limit, cuts=(), held_as=jnp.bfloat16):
    entries = jax.random.normal(rng, dims, jnp.float32) * width
    if len(cuts) > 0:
        entries = shard_levels(rng, dims, cuts, -0.22, 0.18) * entries
    return jnp.clip(entries, min=-limit, max=limit).astype(held_as)


def setup_inputs(seed: int = 0) -> dict:
    key_list = jax.random.split(jax.random.key(seed), 4)
    return {
        "activations": normal_values(key_list[0], (EXAMPLES, LEN, D), 1.0, 6.0, ((0, 32), (1, 16))),
        "out_grads": draw_out_grads(jax.random.fold_in(key_list[3], 71), 0),
        "clip_bound": jnp.clip(jnp.exp(jax.random.uniform(key_list[2], (1,), jnp.float32, math.log(3584.0), math.log(7168.0))), 3584.0, 7168.0),
    }


def reference(activations, out_grads, clip_bound):
    groups = activations.shape[0] // EX_DEV
    acts = activations.reshape(groups, EX_DEV, LEN, D)
    grads = out_grads.reshape(groups, EX_DEV, LEN, QW)

    def one_group(total, pieces):
        group_acts, group_grads = pieces
        weighted = jnp.zeros((D, QW), jnp.float32)
        for member in range(EX_DEV):
            left = group_acts[member].astype(jnp.float32)
            right = group_grads[member].astype(jnp.float32)
            per_example = jnp.dot(left.T, right, precision=lax.Precision.HIGHEST)
            norm_value = jnp.sqrt(jnp.sum(per_example * per_example))
            factor = jnp.minimum(jnp.float32(1.0), clip_bound[0] / (norm_value + 1e-06))
            weighted = weighted + factor * per_example
        return (total + weighted, None)
    start = jnp.zeros((D, QW), jnp.float32)
    clipped_sum, unused = lax.scan(one_group, start, (acts, grads))
    return clipped_sum
```

```python
import math

import jax
import jax.numpy as jnp
from jax import lax
from jax.experimental import pallas as pl
from jax.experimental.pallas import tpu as pltpu
from jax.sharding import PartitionSpec as P

MESH = pl.DeviceIdType.MESH
F32 = jnp.float32
NX, NY, NZL, NZH = 4, 8, 4, 2
HALF = 32
ROWS = 112
TILE = 512
POWER, SHIFT = 11, 120
OFFSET = (0, 1, 3, 2)
OWN, FROM_RIGHT, FROM_LEFT, FAR = 0, 1, 2, 3


def encode(value, bound):
    u = (value.reshape(-1, 8, 256) * (2.0 ** (SHIFT / POWER) / bound)[None]).reshape(value.shape)
    u2 = u * u
    u4 = u2 * u2
    return ((u4 * u4) * (u2 * u)).astype(jnp.bfloat16)


def decode(code, bound):
    code = code.astype(F32)
    size = jnp.exp2(jnp.log(jnp.maximum(jnp.abs(code), 2.0**-126)) * (1.0 / (POWER * math.log(2.0))))
    size = (size.reshape(-1, 8, 256) * (2.0 ** (-SHIFT / POWER) * bound)[None]).reshape(code.shape)
    return jnp.where(code > 0, size, jnp.where(code < 0, -size, 0.0))


def kernel(
    act, grads, clip, out,
    buf, relay, gr, prod, sq, sq_in, top, bound, bound_in, total_out, total_in, sout, sin, yout, yin, zout, zin,
    load_sem, x_s, x_r, f_s, f_r, z_s, z_r, d_s, d_r, n_s, n_r, b_s, b_r, t_s, t_r, s_s, s_r, y_s, y_r, w_s, w_r,
):
    dp, tp = lax.axis_index("dp"), lax.axis_index("tp")
    y, zl = lax.div(dp, 4), lax.rem(dp, 4)
    zh, x, c = lax.div(tp, 8), lax.rem(lax.div(tp, 2), 4), lax.rem(tp, 2)
    z = zh * 4 + zl

    def peer(dx=0, dy=0, dz=0, dc=0):
        nz = lax.rem(z + dz, 8)
        return (
            lax.rem(y + dy, 8) * 4 + lax.rem(nz, 4),
            lax.div(nz, 4) * 8 + lax.rem(x + dx, 4) * 2 + lax.rem(c + dc, 2),
        )

    def line(r):
        return (y * 4 + lax.rem(zl + r, 4), tp)

    tp_peers = [(i, peer(dx=(i // 2) % 4, dz=4 * (i // 8), dc=i % 2)) for i in range(1, 16)]
    z_far = {0: peer(dz=2), 1: peer(dz=6)}
    x_next = {0: peer(dx=1), 1: peer(dx=3)}
    y_next = {0: peer(dy=1), 1: peer(dy=7)}
    other = peer(dc=1)

    def unit(e, far, pos, core, h):
        return buf.at[e, 16 * far + 4 * pos + 2 * core + h]

    def remote(src, dst, s, r, to):
        return pltpu.make_async_remote_copy(
            src_ref=src, dst_ref=dst, send_sem=s, recv_sem=r, device_id=to, device_id_type=MESH
        )

    started = []

    def start(copy):
        copy.start()
        started.append(copy)

    def x_copy(e, far, d, h):
        return remote(
            unit(e, far, OWN, 0, h), unit(e, far, FROM_LEFT if d == 0 else FROM_RIGHT, 0, h),
            x_s.at[e, far, d, h], x_r.at[e, far, d, h], x_next[d],
        )

    def f_copy(e, far, d):
        return remote(
            unit(e, far, FROM_LEFT if d == 0 else FROM_RIGHT, 0, d), unit(e, far, FAR, 0, d),
            f_s.at[e, far, d], f_r.at[e, far, d], x_next[d],
        )

    def z_copy(e, d, leg):
        src = unit(e, 0, OWN, 0, d) if leg == 0 else relay.at[e, d]
        dst = relay.at[e, d] if leg == 0 else unit(e, 1, OWN, 0, d)
        return remote(src, dst, z_s.at[e, d, leg], z_r.at[e, d, leg], z_far[d])

    def d_copy(e, far, pos, h):
        return remote(
            unit(e, far, pos, 0, h), unit(e, far, pos, 1, h),
            d_s.at[e, far, pos, h], d_r.at[e, far, pos, h], other,
        )

    loads = {
        (e, h): pltpu.make_async_copy(
            act.at[e, pl.ds(h * HALF, HALF)], unit(e, 0, OWN, 0, h), load_sem.at[e, h]
        )
        for e in range(2) for h in range(2)
    }
    for load in loads.values():
        load.start()

    barrier = pltpu.get_barrier_semaphore()
    greeted = [to for _, to in tp_peers] + list(z_far.values())
    greeted += [peer(dy=k) for k in range(1, 8)] + [line(r) for r in range(1, 4)]
    for to in greeted:
        pl.semaphore_signal(barrier, inc=1, device_id=to, device_id_type=MESH)
    pl.semaphore_wait(barrier, len(greeted))

    for e in range(2):
        for h in range(2):
            loads[e, h].wait()
        if e == 0:
            start(z_copy(0, 0, 0))
            start(z_copy(0, 1, 0))
        for h in range(2):
            for d in range(2):
                start(x_copy(e, 0, d, h if d == 0 else 1 - h))
        for h in range(2):
            start(d_copy(e, 0, OWN, h))

    for e in range(2):
        for far in range(2):
            for pos in range(4):
                for core in range(2):
                    block = (
                        lax.rem(zh + far, 2) * 8 + lax.rem(x + OFFSET[pos], 4) * 2 + lax.rem(c + core, 2)
                    )
                    rows = pl.ds(pl.multiple_of(block * 64, 64), 64)
                    gr[e, 8 * far + 2 * pos + core] = grads[e, rows, :]

    def pass_relay(e):
        for d in range(2):
            z_copy(e, d, 0).wait_recv()
            start(z_copy(e, d, 1))

    def take_z(e):
        for d in range(2):
            z_copy(e, d, 1).wait_recv()
            for k in range(2):
                start(x_copy(e, 1, k, d))
            start(d_copy(e, 1, OWN, d))

    def take_x(e, far):
        for step in range(2):
            for d in range(2):
                h = d if step == 0 else 1 - d
                x_copy(e, far, d, h).wait_recv()
                if step == 0:
                    start(f_copy(e, far, d))
                start(d_copy(e, far, FROM_LEFT if d == 0 else FROM_RIGHT, h))

    def take_far(e, far):
        for d in range(2):
            f_copy(e, far, d).wait_recv()
            start(d_copy(e, far, FAR, d))

    def wait_core(e, far, positions):
        for pos in positions:
            for h in range(2):
                d_copy(e, far, pos, h).wait_recv()

    def multiply(e, lo, hi):
        first, last = lo == 0, hi == 8
        k = (hi - lo) * 128
        right = gr[e, 2 * lo:2 * hi].reshape(k, 256)

        def body(j, state):
            total, most = state
            cols = pl.ds(pl.multiple_of(j * TILE, TILE), TILE)
            left = buf[e, 4 * lo:4 * hi, :, cols].reshape(k, TILE)
            part = lax.dot_general(left, right, (((0,), (0,)), ((), ())), preferred_element_type=F32)
            if not first:
                part = part + prod[e, cols, :]
            prod[e, cols, :] = part
            if last:
                total = total + jnp.sum((part * part).reshape(TILE // 8, 8, 256), axis=0)
                most = jnp.maximum(most, jnp.max(jnp.abs(part).reshape(TILE // 8, 8, 256), axis=0))
            return total, most

        none = jnp.zeros((8, 256), F32)
        total, most = lax.fori_loop(0, 3584 // TILE, body, (none, none))
        if last:
            sq[e] = total
            top[e] = most
            for i, to in tp_peers:
                start(remote(sq.at[e], sq_in.at[e, i], n_s.at[e, i], n_r.at[e, i], to))

    def begins(d, r):
        return 4 if (r in (1, 3)) == (d == 0) else 3

    def block(e, row_y, r):
        rows = pl.ds(pl.multiple_of((row_y * 4 + lax.rem(zl + r, 4)) * ROWS, 16), ROWS)
        return prod[e, rows, :]

    def ahead(d, dist):
        return lax.rem(y + (dist if d == 0 else 8 - dist), 8)

    def tile_max(value):
        return jnp.broadcast_to(jnp.max(value, axis=(0, 1), keepdims=True), (8, 256))

    order = [(0, 1), (1, 2), (0, 3), (1, 0), (1, 1), (0, 2), (1, 3), (0, 0)]

    def s_copy(e, d, r):
        return remote(sout.at[e, d, r], sin.at[e, d, r], s_s.at[e, d, r], s_r.at[e, d, r], y_next[d])

    def first_hop(e):
        most = tile_max(top[e]) * 1.0001 + 1e-35
        for d, r in order:
            sout[e, d, r] = encode(block(e, ahead(d, begins(d, r)), r), most)
            start(s_copy(e, d, r))
        return most

    def factor(e):
        total = sq[e]
        for i, to in tp_peers:
            remote(sq.at[e], sq_in.at[e, i], n_s.at[e, i], n_r.at[e, i], to).wait_recv()
            total = total + sq_in[e, i]
        norm = jnp.sqrt(jnp.broadcast_to(jnp.sum(total, axis=(0, 1), keepdims=True), (8, 256)))
        return jnp.minimum(1.0, clip[0] / (norm + 1e-06))

    def b_copy(e, k):
        return remote(bound.at[e], bound_in.at[e, k], b_s.at[e, k], b_r.at[e, k], peer(dy=k))

    def send_bound(e, value):
        bound[e] = value
        for k in (1, 7, 2, 6, 3, 5, 4):
            start(b_copy(e, k))

    pass_relay(0)
    take_x(0, 0)
    take_x(1, 0)
    take_z(0)
    start(z_copy(1, 0, 0))
    start(z_copy(1, 1, 0))
    for e in range(2):
        wait_core(e, 0, [OWN, FROM_RIGHT, FROM_LEFT])
        multiply(e, 0, 3)
    pass_relay(1)
    take_far(0, 0)
    take_far(1, 0)
    take_x(0, 1)
    take_z(1)
    wait_core(0, 0, [FAR])
    wait_core(0, 1, [OWN, FROM_RIGHT, FROM_LEFT])
    multiply(0, 3, 7)
    wait_core(1, 0, [FAR])
    wait_core(1, 1, [OWN])
    multiply(1, 3, 5)
    take_far(0, 1)
    wait_core(0, 1, [FAR])
    multiply(0, 7, 8)
    most0 = first_hop(0)
    take_x(1, 1)
    wait_core(1, 1, [FROM_RIGHT, FROM_LEFT])
    multiply(1, 5, 7)
    factor0 = factor(0)
    bound0 = factor0 * most0
    send_bound(0, bound0)
    take_far(1, 1)
    wait_core(1, 1, [FAR])
    multiply(1, 7, 8)
    most1 = first_hop(1)
    factor1 = factor(1)
    bound1 = factor1 * most1
    send_bound(1, bound1)
    mine = bound0 + bound1

    def own(row_y, r):
        terms = [
            scale[None] * block(e, row_y, r).reshape(ROWS // 8, 8, 256)
            for e, scale in enumerate((factor0, factor1))
        ]
        return (terms[0] + terms[1]).reshape(ROWS, 256)

    def t_copy(r):
        return remote(total_out, total_in.at[r], t_s.at[r], t_r.at[r], line(r))

    def y_copy(d, dist, r):
        return remote(
            yout.at[d, dist - 1, r], yin.at[d, dist - 1, r],
            y_s.at[d, dist - 1, r], y_r.at[d, dist - 1, r], y_next[d],
        )

    sums = {}

    def take_bound(d, n):
        k = n if d == 0 else 8 - n
        if not (d == 1 and n == 4):
            for e in range(2):
                b_copy(e, k).wait_recv()
        near = bound_in[0, k] + bound_in[1, k]
        sums[d, n] = near if n == 1 else sums[d, n - 1] + near

    def arrived(d, dist, r):
        steps = begins(d, r) - dist
        if steps > 1:
            y_copy(d, dist + 1, r).wait_recv()
            return decode(yin[d, dist, r], sums[d, steps])
        value = 0.0
        for e in range(2):
            s_copy(e, d, r).wait_recv()
            value = value + decode(sin[e, d, r], bound_in[e, 1 if d == 0 else 7])
        return value

    for steps in (1, 2, 3):
        for d in range(2):
            if (d, steps) not in sums:
                take_bound(d, steps)
        for d, r in order:
            dist = begins(d, r) - steps
            if dist > 0:
                value = own(ahead(d, dist), r) + arrived(d, dist, r)
                yout[d, dist - 1, r] = encode(value, mine + sums[d, steps])
                start(y_copy(d, dist, r))
        if steps == 2:
            for n in (3, 4):
                for d in range(2):
                    if (d, n) not in sums:
                        take_bound(d, n)
            total_out[...] = mine + sums[0, 4] + sums[1, 3]
            for r in range(1, 4):
                start(t_copy(r))

    def w_copy(r):
        return remote(zout.at[r], zin.at[r], w_s.at[r], w_r.at[r], line(r))

    result = None
    for r in (1, 2, 3, 0):
        value = own(y, r)
        for d in range(2):
            value = value + arrived(d, 0, r)
        if r == 0:
            result = value
        else:
            zout[r] = encode(value, total_out[...])
            start(w_copy(r))
    for r in range(1, 4):
        t_copy(r).wait_recv()
        w_copy(r).wait_recv()
        result = result + decode(zin[r], total_in[r])
    out[...] = result
    for copy in started:
        copy.wait_send()


def body(activations, out_grads, clip_bound):
    vmem, dma = pltpu.VMEM, pltpu.SemaphoreType.DMA
    return pl.pallas_call(
        kernel,
        out_shape=jax.ShapeDtypeStruct((ROWS, 256), F32),
        in_specs=[
            pl.BlockSpec(memory_space=pl.ANY),
            pl.BlockSpec(memory_space=pltpu.VMEM),
            pl.BlockSpec(memory_space=pltpu.SMEM),
        ],
        out_specs=pl.BlockSpec(memory_space=pltpu.VMEM),
        scratch_shapes=[
            vmem((2, 32, HALF, 3584), jnp.bfloat16),
            vmem((2, 2, HALF, 3584), jnp.bfloat16),
            vmem((2, 16, 64, 256), jnp.bfloat16),
            vmem((2, 3584, 256), F32),
            vmem((2, 8, 256), F32),
            vmem((2, 16, 8, 256), F32),
            vmem((2, 8, 256), F32),
            vmem((2, 8, 256), F32),
            vmem((2, 8, 8, 256), F32),
            vmem((8, 256), F32),
            vmem((4, 8, 256), F32),
            vmem((2, 2, 4, ROWS, 256), jnp.bfloat16),
            vmem((2, 2, 4, ROWS, 256), jnp.bfloat16),
            vmem((2, 3, 4, ROWS, 256), jnp.bfloat16),
            vmem((2, 3, 4, ROWS, 256), jnp.bfloat16),
            vmem((4, ROWS, 256), jnp.bfloat16),
            vmem((4, ROWS, 256), jnp.bfloat16),
            dma((2, 2)),
            dma((2, 2, 2, 2)), dma((2, 2, 2, 2)),
            dma((2, 2, 2)), dma((2, 2, 2)),
            dma((2, 2, 2)), dma((2, 2, 2)),
            dma((2, 2, 4, 2)), dma((2, 2, 4, 2)),
            dma((2, 16)), dma((2, 16)),
            dma((2, 8)), dma((2, 8)),
            dma((4,)), dma((4,)),
            dma((2, 2, 4)), dma((2, 2, 4)),
            dma((2, 3, 4)), dma((2, 3, 4)),
            dma((4,)), dma((4,)),
        ],
        compiler_params=pltpu.CompilerParams(
            collective_id=0, has_side_effects=True, vmem_limit_bytes=56 * 2**20
        ),
        cost_estimate=pl.CostEstimate(flops=3758096384, bytes_accessed=20000000, transcendentals=1000000),
    )(activations, out_grads, clip_bound)


def solution(mesh):
    return jax.shard_map(
        body,
        mesh=mesh,
        in_specs=(P("dp", "tp", None), P("dp", None, "tp"), P()),
        out_specs=P("dp", "tp"),
        check_vma=False,
    )
```

```python
import math

import jax
import jax.numpy as jnp
from jax import lax
from jax.experimental import pallas as pl
from jax.experimental.pallas import tpu as pltpu
from jax.sharding import PartitionSpec as P

MESH = pl.DeviceIdType.MESH
F32 = jnp.float32
NX, NY, NZL, NZH = 4, 8, 4, 2
HALF = 32
ROWS = 112
TILE = 512
POWER, SHIFT = 11, 120
OFFSET = (0, 1, 3, 2)
OWN, FROM_RIGHT, FROM_LEFT, FAR = 0, 1, 2, 3


def encode(value, bound):
    u = (value.reshape(-1, 8, 256) * (2.0 ** (SHIFT / POWER) / bound)[None]).reshape(value.shape)
    u2 = u * u
    u4 = u2 * u2
    return ((u4 * u4) * (u2 * u)).astype(jnp.bfloat16)


def decode(code, bound):
    code = code.astype(F32)
    size = jnp.exp2(jnp.log(jnp.maximum(jnp.abs(code), 2.0**-126)) * (1.0 / (POWER * math.log(2.0))))
    size = (size.reshape(-1, 8, 256) * (2.0 ** (-SHIFT / POWER) * bound)[None]).reshape(code.shape)
    return jnp.where(code > 0, size, jnp.where(code < 0, -size, 0.0))


def kernel(
    act, grads_in, clip, out,
    grads, buf, relay, gr, prod, sq, sq_in, top, bound, bound_in, total_out, total_in, sout, sin, yout, yin, zout, zin,
    load_sem, grads_sem, x_s, x_r, f_s, f_r, z_s, z_r, d_s, d_r, n_s, n_r, b_s, b_r, t_s, t_r, s_s, s_r, y_s, y_r, w_s, w_r,
):
    dp, tp = lax.axis_index("dp"), lax.axis_index("tp")
    y, zl = lax.div(dp, 4), lax.rem(dp, 4)
    zh, x, c = lax.div(tp, 8), lax.rem(lax.div(tp, 2), 4), lax.rem(tp, 2)
    z = zh * 4 + zl

    def peer(dx=0, dy=0, dz=0, dc=0):
        nz = lax.rem(z + dz, 8)
        return (
            lax.rem(y + dy, 8) * 4 + lax.rem(nz, 4),
            lax.div(nz, 4) * 8 + lax.rem(x + dx, 4) * 2 + lax.rem(c + dc, 2),
        )

    def line(r):
        return (y * 4 + lax.rem(zl + r, 4), tp)

    tp_peers = [(i, peer(dx=(i // 2) % 4, dz=4 * (i // 8), dc=i % 2)) for i in range(1, 16)]
    z_far = {0: peer(dz=2), 1: peer(dz=6)}
    x_next = {0: peer(dx=1), 1: peer(dx=3)}
    y_next = {0: peer(dy=1), 1: peer(dy=7)}
    other = peer(dc=1)

    def unit(e, far, pos, core, h):
        return buf.at[e, 16 * far + 4 * pos + 2 * core + h]

    def remote(src, dst, s, r, to):
        return pltpu.make_async_remote_copy(
            src_ref=src, dst_ref=dst, send_sem=s, recv_sem=r, device_id=to, device_id_type=MESH
        )

    started = []

    def settle(count):
        for copy in started[:count]:
            copy.wait_send()
        del started[:count]

    def start(copy):
        copy.start()
        started.append(copy)

    def x_copy(e, far, d, h):
        return remote(
            unit(e, far, OWN, 0, h), unit(e, far, FROM_LEFT if d == 0 else FROM_RIGHT, 0, h),
            x_s.at[e, far, d, h], x_r.at[e, far, d, h], x_next[d],
        )

    def f_copy(e, far, d):
        return remote(
            unit(e, far, FROM_LEFT if d == 0 else FROM_RIGHT, 0, d), unit(e, far, FAR, 0, d),
            f_s.at[e, far, d], f_r.at[e, far, d], x_next[d],
        )

    def z_copy(e, d, leg):
        src = unit(e, 0, OWN, 0, d) if leg == 0 else relay.at[e, d]
        dst = relay.at[e, d] if leg == 0 else unit(e, 1, OWN, 0, d)
        return remote(src, dst, z_s.at[e, d, leg], z_r.at[e, d, leg], z_far[d])

    def d_copy(e, far, pos, h):
        return remote(
            unit(e, far, pos, 0, h), unit(e, far, pos, 1, h),
            d_s.at[e, far, pos, h], d_r.at[e, far, pos, h], other,
        )

    loads = {
        (e, h): pltpu.make_async_copy(
            act.at[e, pl.ds(h * HALF, HALF)], unit(e, 0, OWN, 0, h), load_sem.at[e, h]
        )
        for e in range(2) for h in range(2)
    }
    for load in loads.values():
        load.start()
    grads_load = pltpu.make_async_copy(grads_in, grads, grads_sem)
    grads_load.start()

    barrier = pltpu.get_barrier_semaphore()
    greeted = [to for _, to in tp_peers] + list(z_far.values())
    greeted += [peer(dy=k) for k in range(1, 8)] + [line(r) for r in range(1, 4)]
    for to in greeted:
        pl.semaphore_signal(barrier, inc=1, device_id=to, device_id_type=MESH)
    pl.semaphore_wait(barrier, len(greeted))

    for e in range(2):
        for h in range(2):
            loads[e, h].wait()
        if e == 0:
            start(z_copy(0, 0, 0))
            start(z_copy(0, 1, 0))
        for h in range(2):
            for d in range(2):
                start(x_copy(e, 0, d, h if d == 0 else 1 - h))
        for h in range(2):
            start(d_copy(e, 0, OWN, h))

    grads_load.wait()
    for e in range(2):
        for far in range(2):
            for pos in range(4):
                for core in range(2):
                    block = (
                        lax.rem(zh + far, 2) * 8 + lax.rem(x + OFFSET[pos], 4) * 2 + lax.rem(c + core, 2)
                    )
                    rows = pl.ds(pl.multiple_of(block * 64, 64), 64)
                    gr[e, 8 * far + 2 * pos + core] = grads[e, rows, :]

    def pass_relay(e):
        for d in range(2):
            z_copy(e, d, 0).wait_recv()
            start(z_copy(e, d, 1))

    def take_z(e):
        for d in range(2):
            z_copy(e, d, 1).wait_recv()
            for k in range(2):
                start(x_copy(e, 1, k, d))
            start(d_copy(e, 1, OWN, d))

    def take_x(e, far):
        for step in range(2):
            for d in range(2):
                h = d if step == 0 else 1 - d
                x_copy(e, far, d, h).wait_recv()
                if step == 0:
                    start(f_copy(e, far, d))
                start(d_copy(e, far, FROM_LEFT if d == 0 else FROM_RIGHT, h))

    def take_far(e, far):
        for d in range(2):
            f_copy(e, far, d).wait_recv()
            start(d_copy(e, far, FAR, d))

    def wait_core(e, far, positions):
        for pos in positions:
            for h in range(2):
                d_copy(e, far, pos, h).wait_recv()

    def multiply(e, lo, hi):
        first, last = lo == 0, hi == 8
        k = (hi - lo) * 128
        right = gr[e, 2 * lo:2 * hi].reshape(k, 256)

        def body(j, state):
            total, most = state
            cols = pl.ds(pl.multiple_of(j * TILE, TILE), TILE)
            left = buf[e, 4 * lo:4 * hi, :, cols].reshape(k, TILE)
            part = lax.dot_general(left, right, (((0,), (0,)), ((), ())), preferred_element_type=F32)
            if not first:
                part = part + prod[e, cols, :]
            prod[e, cols, :] = part
            if last:
                total = total + jnp.sum((part * part).reshape(TILE // 8, 8, 256), axis=0)
                most = jnp.maximum(most, jnp.max(jnp.abs(part).reshape(TILE // 8, 8, 256), axis=0))
            return total, most

        none = jnp.zeros((8, 256), F32)
        total, most = lax.fori_loop(0, 3584 // TILE, body, (none, none))
        if last:
            sq[e] = total
            top[e] = most
            for i, to in tp_peers:
                start(remote(sq.at[e], sq_in.at[e, i], n_s.at[e, i], n_r.at[e, i], to))

    def begins(d, r):
        return 4 if (r in (1, 3)) == (d == 0) else 3

    def block(e, row_y, r):
        rows = pl.ds(pl.multiple_of((row_y * 4 + lax.rem(zl + r, 4)) * ROWS, 16), ROWS)
        return prod[e, rows, :]

    def ahead(d, dist):
        return lax.rem(y + (dist if d == 0 else 8 - dist), 8)

    def tile_max(value):
        return jnp.broadcast_to(jnp.max(value, axis=(0, 1), keepdims=True), (8, 256))

    order = [(0, 1), (1, 2), (0, 3), (1, 0), (1, 1), (0, 2), (1, 3), (0, 0)]

    def s_copy(e, d, r):
        return remote(sout.at[e, d, r], sin.at[e, d, r], s_s.at[e, d, r], s_r.at[e, d, r], y_next[d])

    def first_hop(e):
        most = tile_max(top[e]) * 1.0001 + 1e-35
        for d, r in order:
            sout[e, d, r] = encode(block(e, ahead(d, begins(d, r)), r), most)
            start(s_copy(e, d, r))
        return most

    def factor(e):
        total = sq[e]
        for i, to in tp_peers:
            remote(sq.at[e], sq_in.at[e, i], n_s.at[e, i], n_r.at[e, i], to).wait_recv()
            total = total + sq_in[e, i]
        norm = jnp.sqrt(jnp.broadcast_to(jnp.sum(total, axis=(0, 1), keepdims=True), (8, 256)))
        return jnp.minimum(1.0, clip[0] / (norm + 1e-06))

    def b_copy(e, k):
        return remote(bound.at[e], bound_in.at[e, k], b_s.at[e, k], b_r.at[e, k], peer(dy=k))

    def send_bound(e, value):
        bound[e] = value
        for k in (1, 7, 2, 6, 3, 5, 4):
            start(b_copy(e, k))

    pass_relay(0)
    take_x(0, 0)
    take_x(1, 0)
    take_z(0)
    start(z_copy(1, 0, 0))
    start(z_copy(1, 1, 0))
    for e in range(2):
        wait_core(e, 0, [OWN, FROM_RIGHT, FROM_LEFT])
        multiply(e, 0, 3)
    pass_relay(1)
    take_far(0, 0)
    take_far(1, 0)
    take_x(0, 1)
    take_z(1)
    wait_core(0, 0, [FAR])
    wait_core(0, 1, [OWN, FROM_RIGHT, FROM_LEFT])
    multiply(0, 3, 7)
    take_far(0, 1)
    wait_core(0, 1, [FAR])
    multiply(0, 7, 8)
    take_x(1, 1)
    most0 = first_hop(0)
    wait_core(1, 0, [FAR])
    wait_core(1, 1, [OWN, FROM_RIGHT, FROM_LEFT])
    multiply(1, 3, 7)
    factor0 = factor(0)
    bound0 = factor0 * most0
    send_bound(0, bound0)
    take_far(1, 1)
    gathered = len(started)
    wait_core(1, 1, [FAR])
    multiply(1, 7, 8)
    most1 = first_hop(1)
    settle(gathered)
    factor1 = factor(1)
    bound1 = factor1 * most1
    send_bound(1, bound1)
    mine = bound0 + bound1

    def own(row_y, r):
        terms = [
            scale[None] * block(e, row_y, r).reshape(ROWS // 8, 8, 256)
            for e, scale in enumerate((factor0, factor1))
        ]
        return (terms[0] + terms[1]).reshape(ROWS, 256)

    def t_copy(r):
        return remote(total_out, total_in.at[r], t_s.at[r], t_r.at[r], line(r))

    def y_copy(d, dist, r):
        return remote(
            yout.at[d, dist - 1, r], yin.at[d, dist - 1, r],
            y_s.at[d, dist - 1, r], y_r.at[d, dist - 1, r], y_next[d],
        )

    sums = {}

    def take_bound(d, n):
        k = n if d == 0 else 8 - n
        if not (d == 1 and n == 4):
            for e in range(2):
                b_copy(e, k).wait_recv()
        near = bound_in[0, k] + bound_in[1, k]
        sums[d, n] = near if n == 1 else sums[d, n - 1] + near

    def arrived(d, dist, r):
        steps = begins(d, r) - dist
        if steps > 1:
            y_copy(d, dist + 1, r).wait_recv()
            return decode(yin[d, dist, r], sums[d, steps])
        value = 0.0
        for e in range(2):
            s_copy(e, d, r).wait_recv()
            value = value + decode(sin[e, d, r], bound_in[e, 1 if d == 0 else 7])
        return value

    def w_copy(r):
        return remote(zout.at[r], zin.at[r], w_s.at[r], w_r.at[r], line(r))

    def pass_on(steps, rows):
        for d in range(2):
            if (d, steps) not in sums:
                take_bound(d, steps)
        for d, r in order:
            dist = begins(d, r) - steps
            if r in rows and dist > 0:
                value = own(ahead(d, dist), r) + arrived(d, dist, r)
                yout[d, dist - 1, r] = encode(value, mine + sums[d, steps])
                start(y_copy(d, dist, r))

    def reduced(r):
        value = own(y, r)
        for d in range(2):
            value = value + arrived(d, 0, r)
        return value

    others = (1, 2, 3)
    pass_on(1, others)
    pass_on(1, (0,))
    pass_on(2, others)
    for n in (3, 4):
        for d in range(2):
            take_bound(d, n)
    total_out[...] = mine + sums[0, 4] + sums[1, 3]
    for r in others:
        start(t_copy(r))
    pass_on(3, others)
    pass_on(2, (0,))
    for r in others:
        zout[r] = encode(reduced(r), total_out[...])
        start(w_copy(r))
    pass_on(3, (0,))
    result = reduced(0)
    for r in others:
        t_copy(r).wait_recv()
        w_copy(r).wait_recv()
        result = result + decode(zin[r], total_in[r])
    out[...] = result
    settle(len(started))


def body(activations, out_grads, clip_bound):
    vmem, dma = pltpu.VMEM, pltpu.SemaphoreType.DMA
    return pl.pallas_call(
        kernel,
        out_shape=jax.ShapeDtypeStruct((ROWS, 256), F32),
        in_specs=[
            pl.BlockSpec(memory_space=pl.ANY),
            pl.BlockSpec(memory_space=pl.ANY),
            pl.BlockSpec(memory_space=pltpu.SMEM),
        ],
        out_specs=pl.BlockSpec(memory_space=pltpu.VMEM),
        scratch_shapes=[
            vmem((2, 1024, 256), jnp.bfloat16),
            vmem((2, 32, HALF, 3584), jnp.bfloat16),
            vmem((2, 2, HALF, 3584), jnp.bfloat16),
            vmem((2, 16, 64, 256), jnp.bfloat16),
            vmem((2, 3584, 256), F32),
            vmem((2, 8, 256), F32),
            vmem((2, 16, 8, 256), F32),
            vmem((2, 8, 256), F32),
            vmem((2, 8, 256), F32),
            vmem((2, 8, 8, 256), F32),
            vmem((8, 256), F32),
            vmem((4, 8, 256), F32),
            vmem((2, 2, 4, ROWS, 256), jnp.bfloat16),
            vmem((2, 2, 4, ROWS, 256), jnp.bfloat16),
            vmem((2, 3, 4, ROWS, 256), jnp.bfloat16),
            vmem((2, 3, 4, ROWS, 256), jnp.bfloat16),
            vmem((4, ROWS, 256), jnp.bfloat16),
            vmem((4, ROWS, 256), jnp.bfloat16),
            dma((2, 2)),
            dma,
            dma((2, 2, 2, 2)), dma((2, 2, 2, 2)),
            dma((2, 2, 2)), dma((2, 2, 2)),
            dma((2, 2, 2)), dma((2, 2, 2)),
            dma((2, 2, 4, 2)), dma((2, 2, 4, 2)),
            dma((2, 16)), dma((2, 16)),
            dma((2, 8)), dma((2, 8)),
            dma((4,)), dma((4,)),
            dma((2, 2, 4)), dma((2, 2, 4)),
            dma((2, 3, 4)), dma((2, 3, 4)),
            dma((4,)), dma((4,)),
        ],
        compiler_params=pltpu.CompilerParams(
            collective_id=0, has_side_effects=True, vmem_limit_bytes=56 * 2**20
        ),
        cost_estimate=pl.CostEstimate(flops=3758096384, bytes_accessed=20000000, transcendentals=1000000),
    )(activations, out_grads, clip_bound)


def solution(mesh):
    return jax.shard_map(
        body,
        mesh=mesh,
        in_specs=(P("dp", "tp", None), P("dp", None, "tp"), P()),
        out_specs=P("dp", "tp"),
        check_vma=False,
    )
```

```python
import math

import jax
import jax.numpy as jnp
from jax import lax
from jax.experimental import pallas as pl
from jax.experimental.pallas import tpu as pltpu
from jax.sharding import PartitionSpec as P

MESH = pl.DeviceIdType.MESH
F32 = jnp.float32
NX, NY, NZL, NZH = 4, 8, 4, 2
HALF = 32
ROWS = 112
TILE = 512
POWER, SHIFT = 11, 120
OFFSET = (0, 1, 3, 2)
OWN, FROM_RIGHT, FROM_LEFT, FAR = 0, 1, 2, 3


def encode(value, bound):
    u = (value.reshape(-1, 8, 256) * (2.0 ** (SHIFT / POWER) / bound)[None]).reshape(value.shape)
    u2 = u * u
    u4 = u2 * u2
    return ((u4 * u4) * (u2 * u)).astype(jnp.bfloat16)


def decode(code, bound):
    code = code.astype(F32)
    size = jnp.exp2(jnp.log(jnp.maximum(jnp.abs(code), 2.0**-126)) * (1.0 / (POWER * math.log(2.0))))
    size = (size.reshape(-1, 8, 256) * (2.0 ** (-SHIFT / POWER) * bound)[None]).reshape(code.shape)
    return jnp.where(code < 0, -size, size)


def kernel(
    act, grads_in, clip, out,
    grads, buf, relay, gr, prod, sq, sq_in, top, bound, bound_in, total_out, total_in, sout, sin, yout, yin, zout, zin,
    load_sem, grads_sem, x_s, x_r, f_s, f_r, z_s, z_r, d_s, d_r, n_s, n_r, b_s, b_r, t_s, t_r, s_s, s_r, y_s, y_r, w_s, w_r,
):
    dp, tp = lax.axis_index("dp"), lax.axis_index("tp")
    y, zl = lax.div(dp, 4), lax.rem(dp, 4)
    zh, x, c = lax.div(tp, 8), lax.rem(lax.div(tp, 2), 4), lax.rem(tp, 2)
    z = zh * 4 + zl

    def peer(dx=0, dy=0, dz=0, dc=0):
        nz = lax.rem(z + dz, 8)
        return (
            lax.rem(y + dy, 8) * 4 + lax.rem(nz, 4),
            lax.div(nz, 4) * 8 + lax.rem(x + dx, 4) * 2 + lax.rem(c + dc, 2),
        )

    def line(r):
        return (y * 4 + lax.rem(zl + r, 4), tp)

    tp_peers = [(i, peer(dx=(i // 2) % 4, dz=4 * (i // 8), dc=i % 2)) for i in range(15, 0, -1)]
    z_far = {0: peer(dz=2), 1: peer(dz=6)}
    x_next = {0: peer(dx=1), 1: peer(dx=3)}
    y_next = {0: peer(dy=1), 1: peer(dy=7)}
    other = peer(dc=1)

    def unit(e, far, pos, core, h):
        return buf.at[e, 16 * far + 4 * pos + 2 * core + h]

    def remote(src, dst, s, r, to):
        return pltpu.make_async_remote_copy(
            src_ref=src, dst_ref=dst, send_sem=s, recv_sem=r, device_id=to, device_id_type=MESH
        )

    started = []

    def settle(count):
        for copy in started[:count]:
            copy.wait_send()
        del started[:count]

    def start(copy):
        copy.start()
        started.append(copy)

    def x_copy(e, far, d, h):
        return remote(
            unit(e, far, OWN, 0, h), unit(e, far, FROM_LEFT if d == 0 else FROM_RIGHT, 0, h),
            x_s.at[e, far, d, h], x_r.at[e, far, d, h], x_next[d],
        )

    def f_copy(e, far, d):
        return remote(
            unit(e, far, FROM_LEFT if d == 0 else FROM_RIGHT, 0, d), unit(e, far, FAR, 0, d),
            f_s.at[e, far, d], f_r.at[e, far, d], x_next[d],
        )

    def z_copy(e, d, leg):
        src = unit(e, 0, OWN, 0, d) if leg == 0 else relay.at[e, d]
        dst = relay.at[e, d] if leg == 0 else unit(e, 1, OWN, 0, d)
        return remote(src, dst, z_s.at[e, d, leg], z_r.at[e, d, leg], z_far[d])

    def d_copy(e, far, pos, h):
        return remote(
            unit(e, far, pos, 0, h), unit(e, far, pos, 1, h),
            d_s.at[e, far, pos, h], d_r.at[e, far, pos, h], other,
        )

    loads = {
        (e, h): pltpu.make_async_copy(
            act.at[e, pl.ds(h * HALF, HALF)], unit(e, 0, OWN, 0, h), load_sem.at[e, h]
        )
        for e in range(2) for h in range(2)
    }
    for load in loads.values():
        load.start()
    grads_load = pltpu.make_async_copy(grads_in, grads, grads_sem)
    grads_load.start()

    barrier = pltpu.get_barrier_semaphore()
    greeted = [to for _, to in tp_peers] + list(z_far.values())
    greeted += [peer(dy=k) for k in range(1, 8)] + [line(r) for r in range(1, 4)]
    for to in greeted:
        pl.semaphore_signal(barrier, inc=1, device_id=to, device_id_type=MESH)
    pl.semaphore_wait(barrier, len(greeted))

    for e in range(2):
        for h in range(2):
            loads[e, h].wait()
        if e == 0:
            start(z_copy(0, 0, 0))
            start(z_copy(0, 1, 0))
        for h in range(2):
            for d in range(2):
                start(x_copy(e, 0, d, h if d == 0 else 1 - h))
        for h in range(2):
            start(d_copy(e, 0, OWN, h))

    grads_load.wait()
    for e in range(2):
        for far in range(2):
            for pos in range(4):
                for core in range(2):
                    block = (
                        lax.rem(zh + far, 2) * 8 + lax.rem(x + OFFSET[pos], 4) * 2 + lax.rem(c + core, 2)
                    )
                    rows = pl.ds(pl.multiple_of(block * 64, 64), 64)
                    gr[e, 8 * far + 2 * pos + core] = grads[e, rows, :]

    def pass_relay(e):
        for d in range(2):
            z_copy(e, d, 0).wait_recv()
            start(z_copy(e, d, 1))

    def take_z(e):
        for d in range(2):
            z_copy(e, d, 1).wait_recv()
            for k in range(2):
                start(x_copy(e, 1, k, d))
            start(d_copy(e, 1, OWN, d))

    def take_x(e, far):
        for step in range(2):
            for d in range(2):
                h = d if step == 0 else 1 - d
                x_copy(e, far, d, h).wait_recv()
                if step == 0:
                    start(f_copy(e, far, d))
                start(d_copy(e, far, FROM_LEFT if d == 0 else FROM_RIGHT, h))

    def take_far(e, far):
        for d in range(2):
            f_copy(e, far, d).wait_recv()
            start(d_copy(e, far, FAR, d))

    def wait_core(e, far, positions):
        for pos in positions:
            for h in range(2):
                d_copy(e, far, pos, h).wait_recv()

    def multiply(e, lo, hi):
        first, last = lo == 0, hi == 8
        k = (hi - lo) * 128
        right = gr[e, 2 * lo:2 * hi].reshape(k, 256)

        def body(j, state):
            total, most = state
            cols = pl.ds(pl.multiple_of(j * TILE, TILE), TILE)
            left = buf[e, 4 * lo:4 * hi, :, cols].reshape(k, TILE)
            part = lax.dot_general(left, right, (((0,), (0,)), ((), ())), preferred_element_type=F32)
            if not first:
                part = part + prod[e, cols, :]
            prod[e, cols, :] = part
            if last:
                total = total + jnp.sum((part * part).reshape(TILE // 8, 8, 256), axis=0)
                most = jnp.maximum(most, jnp.max(jnp.abs(part).reshape(TILE // 8, 8, 256), axis=0))
            return total, most

        none = jnp.zeros((8, 256), F32)
        total, most = lax.fori_loop(0, 3584 // TILE, body, (none, none))
        if last:
            sq[e] = total
            top[e] = most
            for i, to in tp_peers:
                start(remote(sq.at[e], sq_in.at[e, i], n_s.at[e, i], n_r.at[e, i], to))

    def begins(d, r):
        return 4 if (r in (1, 3)) == (d == 0) else 3

    def block(e, row_y, r):
        rows = pl.ds(pl.multiple_of((row_y * 4 + lax.rem(zl + r, 4)) * ROWS, 16), ROWS)
        return prod[e, rows, :]

    def ahead(d, dist):
        return lax.rem(y + (dist if d == 0 else 8 - dist), 8)

    def tile_max(value):
        return jnp.broadcast_to(jnp.max(value, axis=(0, 1), keepdims=True), (8, 256))

    order = [(0, 1), (1, 2), (0, 3), (0, 2), (1, 0), (0, 0), (1, 3), (1, 1)]

    def s_copy(e, d, r):
        return remote(sout.at[e, d, r], sin.at[e, d, r], s_s.at[e, d, r], s_r.at[e, d, r], y_next[d])

    def first_hop(e):
        most = tile_max(top[e]) * 1.0001 + 1e-35
        for d, r in order:
            sout[e, d, r] = encode(block(e, ahead(d, begins(d, r)), r), most)
            start(s_copy(e, d, r))
        return most

    def factor(e):
        total = sq[e]
        for i, to in tp_peers:
            remote(sq.at[e], sq_in.at[e, i], n_s.at[e, i], n_r.at[e, i], to).wait_recv()
            total = total + sq_in[e, i]
        norm = jnp.sqrt(jnp.broadcast_to(jnp.sum(total, axis=(0, 1), keepdims=True), (8, 256)))
        return jnp.minimum(1.0, clip[0] / (norm + 1e-06))

    def b_copy(e, k):
        return remote(bound.at[e], bound_in.at[e, k], b_s.at[e, k], b_r.at[e, k], peer(dy=k))

    def send_bound(e, value):
        bound[e] = value
        for k in (1, 7, 2, 6, 3, 5, 4):
            start(b_copy(e, k))

    pass_relay(0)
    take_x(0, 0)
    take_x(1, 0)
    take_z(0)
    start(z_copy(1, 0, 0))
    start(z_copy(1, 1, 0))
    wait_core(0, 0, [OWN, FROM_RIGHT, FROM_LEFT])
    multiply(0, 0, 3)
    pass_relay(1)
    wait_core(1, 0, [OWN, FROM_RIGHT, FROM_LEFT])
    multiply(1, 0, 3)
    take_far(0, 0)
    take_far(1, 0)
    take_x(0, 1)
    take_z(1)
    wait_core(0, 0, [FAR])
    wait_core(0, 1, [OWN, FROM_RIGHT, FROM_LEFT])
    multiply(0, 3, 7)
    take_far(0, 1)
    wait_core(0, 1, [FAR])
    multiply(0, 7, 8)
    wait_core(1, 0, [FAR])
    wait_core(1, 1, [OWN])
    multiply(1, 3, 5)
    take_x(1, 1)
    most0 = first_hop(0)
    wait_core(1, 1, [FROM_RIGHT, FROM_LEFT])
    multiply(1, 5, 7)
    factor0 = factor(0)
    bound0 = factor0 * most0
    send_bound(0, bound0)
    take_far(1, 1)
    wait_core(1, 1, [FAR])
    multiply(1, 7, 8)
    most1 = first_hop(1)
    factor1 = factor(1)
    bound1 = factor1 * most1
    send_bound(1, bound1)
    mine = bound0 + bound1

    def own(row_y, r):
        terms = [
            scale[None] * block(e, row_y, r).reshape(ROWS // 8, 8, 256)
            for e, scale in enumerate((factor0, factor1))
        ]
        return (terms[0] + terms[1]).reshape(ROWS, 256)

    def t_copy(r):
        return remote(total_out, total_in.at[r], t_s.at[r], t_r.at[r], line(r))

    def y_copy(d, dist, r):
        return remote(
            yout.at[d, dist - 1, r], yin.at[d, dist - 1, r],
            y_s.at[d, dist - 1, r], y_r.at[d, dist - 1, r], y_next[d],
        )

    bounds, sums = {}, {}

    def near(k):
        if k not in bounds:
            for e in range(2):
                b_copy(e, k).wait_recv()
            bounds[k] = bound_in[0, k] + bound_in[1, k]
        return bounds[k]

    def near_sum(d, n):
        if (d, n) not in sums:
            value = near(n if d == 0 else 8 - n)
            sums[d, n] = value if n == 1 else near_sum(d, n - 1) + value
        return sums[d, n]

    def arrived(d, dist, r):
        steps = begins(d, r) - dist
        if steps > 1:
            y_copy(d, dist + 1, r).wait_recv()
            return decode(yin[d, dist, r], near_sum(d, steps))
        value = 0.0
        for e in range(2):
            s_copy(e, d, r).wait_recv()
            value = value + decode(sin[e, d, r], bound_in[e, 1 if d == 0 else 7])
        return value

    def w_copy(r):
        return remote(zout.at[r], zin.at[r], w_s.at[r], w_r.at[r], line(r))

    def pass_on(steps, d, r):
        dist = begins(d, r) - steps
        limit = mine + near_sum(d, steps)
        value = own(ahead(d, dist), r) + arrived(d, dist, r)
        yout[d, dist - 1, r] = encode(value, limit)
        start(y_copy(d, dist, r))

    def reduced(r):
        value = own(y, r)
        for d in range(2):
            value = value + arrived(d, 0, r)
        return value

    def send_reduced(r):
        zout[r] = encode(reduced(r), total_out[...])
        start(w_copy(r))

    for steps, d, r in ((1, 0, 1), (1, 1, 2), (1, 0, 3), (1, 1, 1), (2, 0, 1), (2, 1, 2), (1, 0, 2), (1, 1, 3)):
        pass_on(steps, d, r)
    total_out[...] = mine + near_sum(0, 4) + near_sum(1, 3)
    for r in range(1, 4):
        start(t_copy(r))
    for steps, d, r in ((2, 0, 3), (2, 1, 1), (3, 0, 1), (1, 1, 0), (2, 0, 2), (3, 1, 2), (1, 0, 0), (2, 1, 3), (3, 0, 3)):
        pass_on(steps, d, r)
    send_reduced(1)
    pass_on(2, 1, 0)
    send_reduced(2)
    pass_on(2, 0, 0)
    send_reduced(3)
    pass_on(3, 1, 0)
    result = reduced(0)
    settle(len(started) - 10)
    for r in range(1, 4):
        t_copy(r).wait_recv()
        w_copy(r).wait_recv()
        result = result + decode(zin[r], total_in[r])
    out[...] = result
    settle(len(started))


def body(activations, out_grads, clip_bound):
    vmem, dma = pltpu.VMEM, pltpu.SemaphoreType.DMA
    return pl.pallas_call(
        kernel,
        out_shape=jax.ShapeDtypeStruct((ROWS, 256), F32),
        in_specs=[
            pl.BlockSpec(memory_space=pl.ANY),
            pl.BlockSpec(memory_space=pl.ANY),
            pl.BlockSpec(memory_space=pltpu.SMEM),
        ],
        out_specs=pl.BlockSpec(memory_space=pltpu.VMEM),
        scratch_shapes=[
            vmem((2, 1024, 256), jnp.bfloat16),
            vmem((2, 32, HALF, 3584), jnp.bfloat16),
            vmem((2, 2, HALF, 3584), jnp.bfloat16),
            vmem((2, 16, 64, 256), jnp.bfloat16),
            vmem((2, 3584, 256), F32),
            vmem((2, 8, 256), F32),
            vmem((2, 16, 8, 256), F32),
            vmem((2, 8, 256), F32),
            vmem((2, 8, 256), F32),
            vmem((2, 8, 8, 256), F32),
            vmem((8, 256), F32),
            vmem((4, 8, 256), F32),
            vmem((2, 2, 4, ROWS, 256), jnp.bfloat16),
            vmem((2, 2, 4, ROWS, 256), jnp.bfloat16),
            vmem((2, 3, 4, ROWS, 256), jnp.bfloat16),
            vmem((2, 3, 4, ROWS, 256), jnp.bfloat16),
            vmem((4, ROWS, 256), jnp.bfloat16),
            vmem((4, ROWS, 256), jnp.bfloat16),
            dma((2, 2)),
            dma,
            dma((2, 2, 2, 2)), dma((2, 2, 2, 2)),
            dma((2, 2, 2)), dma((2, 2, 2)),
            dma((2, 2, 2)), dma((2, 2, 2)),
            dma((2, 2, 4, 2)), dma((2, 2, 4, 2)),
            dma((2, 16)), dma((2, 16)),
            dma((2, 8)), dma((2, 8)),
            dma((4,)), dma((4,)),
            dma((2, 2, 4)), dma((2, 2, 4)),
            dma((2, 3, 4)), dma((2, 3, 4)),
            dma((4,)), dma((4,)),
        ],
        compiler_params=pltpu.CompilerParams(
            collective_id=0, has_side_effects=True, vmem_limit_bytes=56 * 2**20
        ),
        cost_estimate=pl.CostEstimate(flops=3758096384, bytes_accessed=20000000, transcendentals=1000000),
    )(activations, out_grads, clip_bound)


def solution(mesh):
    return jax.shard_map(
        body,
        mesh=mesh,
        in_specs=(P("dp", "tp", None), P("dp", None, "tp"), P()),
        out_specs=P("dp", "tp"),
        check_vma=False,
    )
```

```python
import math

import jax
import jax.numpy as jnp
from jax import lax
from jax.experimental import pallas as pl
from jax.experimental.pallas import tpu as pltpu
from jax.sharding import PartitionSpec as P

MESH = pl.DeviceIdType.MESH
F32 = jnp.float32
NX, NY, NZL, NZH = 4, 8, 4, 2
HALF = 32
ROWS = 112
TILE = 512
POWER, SHIFT = 11, 120
OFFSET = (0, 1, 3, 2)
OWN, FROM_RIGHT, FROM_LEFT, FAR = 0, 1, 2, 3


def encode(value, bound):
    u = (value.reshape(-1, 8, 256) * (2.0 ** (SHIFT / POWER) / bound)[None]).reshape(value.shape)
    u2 = u * u
    u4 = u2 * u2
    return ((u4 * u4) * (u2 * u)).astype(jnp.bfloat16)


def decode(code, bound):
    code = code.astype(F32)
    size = jnp.exp2(jnp.log(jnp.maximum(jnp.abs(code), 2.0**-126)) * (1.0 / (POWER * math.log(2.0))))
    size = (size.reshape(-1, 8, 256) * (2.0 ** (-SHIFT / POWER) * bound)[None]).reshape(code.shape)
    return jnp.where(code < 0, -size, size)


def kernel(
    act, grads_in, clip, out,
    grads, buf, relay, gr, prod, sq, sq_in, top, bound, bound_in, line_bound, limit_out, limit_in, sout, sin, yout, yin, zout, zin,
    load_sem, grads_sem, x_s, x_r, f_s, f_r, z_s, z_r, d_s, d_r, n_s, n_r, b_s, b_r, v_s, v_r, t_s, t_r, s_s, s_r, y_s, y_r, w_s, w_r,
):
    dp, tp = lax.axis_index("dp"), lax.axis_index("tp")
    y, zl = lax.div(dp, 4), lax.rem(dp, 4)
    zh, x, c = lax.div(tp, 8), lax.rem(lax.div(tp, 2), 4), lax.rem(tp, 2)
    z = zh * 4 + zl

    def peer(dx=0, dy=0, dz=0, dc=0):
        nz = lax.rem(z + dz, 8)
        return (
            lax.rem(y + dy, 8) * 4 + lax.rem(nz, 4),
            lax.div(nz, 4) * 8 + lax.rem(x + dx, 4) * 2 + lax.rem(c + dc, 2),
        )

    def line(r, dy=0):
        return (lax.rem(y + dy, 8) * 4 + lax.rem(zl + r, 4), tp)

    tp_peers = [(i, peer(dx=(i // 2) % 4, dz=4 * (i // 8), dc=i % 2)) for i in range(15, 0, -1)]
    z_far = {0: peer(dz=2), 1: peer(dz=6)}
    x_next = {0: peer(dx=1), 1: peer(dx=3)}
    y_next = {0: peer(dy=1), 1: peer(dy=7)}
    other = peer(dc=1)

    def unit(e, far, pos, core, h):
        return buf.at[e, 16 * far + 4 * pos + 2 * core + h]

    def remote(src, dst, s, r, to):
        return pltpu.make_async_remote_copy(
            src_ref=src, dst_ref=dst, send_sem=s, recv_sem=r, device_id=to, device_id_type=MESH
        )

    started = []

    def settle(count):
        for copy in started[:count]:
            copy.wait_send()
        del started[:count]

    def start(copy):
        copy.start()
        started.append(copy)

    def x_copy(e, far, d, h):
        return remote(
            unit(e, far, OWN, 0, h), unit(e, far, FROM_LEFT if d == 0 else FROM_RIGHT, 0, h),
            x_s.at[e, far, d, h], x_r.at[e, far, d, h], x_next[d],
        )

    def f_copy(e, far, d):
        return remote(
            unit(e, far, FROM_LEFT if d == 0 else FROM_RIGHT, 0, d), unit(e, far, FAR, 0, d),
            f_s.at[e, far, d], f_r.at[e, far, d], x_next[d],
        )

    def z_copy(e, d, leg):
        src = unit(e, 0, OWN, 0, d) if leg == 0 else relay.at[e, d]
        dst = relay.at[e, d] if leg == 0 else unit(e, 1, OWN, 0, d)
        return remote(src, dst, z_s.at[e, d, leg], z_r.at[e, d, leg], z_far[d])

    def d_copy(e, far, pos, h):
        return remote(
            unit(e, far, pos, 0, h), unit(e, far, pos, 1, h),
            d_s.at[e, far, pos, h], d_r.at[e, far, pos, h], other,
        )

    loads = {
        (e, h): pltpu.make_async_copy(
            act.at[e, pl.ds(h * HALF, HALF)], unit(e, 0, OWN, 0, h), load_sem.at[e, h]
        )
        for e in range(2) for h in range(2)
    }
    for load in loads.values():
        load.start()
    grads_load = pltpu.make_async_copy(grads_in, grads, grads_sem)
    grads_load.start()

    barrier = pltpu.get_barrier_semaphore()
    greeted = [to for _, to in tp_peers] + list(z_far.values())
    greeted += [peer(dy=k) for k in range(1, 8)]
    greeted += [line(r, dy) for r in range(1, 4) for dy in (0, 1, 7)]
    for to in greeted:
        pl.semaphore_signal(barrier, inc=1, device_id=to, device_id_type=MESH)
    pl.semaphore_wait(barrier, len(greeted))

    for e in range(2):
        for h in range(2):
            loads[e, h].wait()
        if e == 0:
            start(z_copy(0, 0, 0))
            start(z_copy(0, 1, 0))
        for h in range(2):
            for d in range(2):
                start(x_copy(e, 0, d, h if d == 0 else 1 - h))
        for h in range(2):
            start(d_copy(e, 0, OWN, h))

    grads_load.wait()
    for e in range(2):
        for far in range(2):
            for pos in range(4):
                for core in range(2):
                    block = (
                        lax.rem(zh + far, 2) * 8 + lax.rem(x + OFFSET[pos], 4) * 2 + lax.rem(c + core, 2)
                    )
                    rows = pl.ds(pl.multiple_of(block * 64, 64), 64)
                    gr[e, 8 * far + 2 * pos + core] = grads[e, rows, :]

    def pass_relay(e):
        for d in range(2):
            z_copy(e, d, 0).wait_recv()
            start(z_copy(e, d, 1))

    def take_z(e):
        for d in range(2):
            z_copy(e, d, 1).wait_recv()
            for k in range(2):
                start(x_copy(e, 1, k, d))
            start(d_copy(e, 1, OWN, d))

    def take_x(e, far):
        for step in range(2):
            for d in range(2):
                h = d if step == 0 else 1 - d
                x_copy(e, far, d, h).wait_recv()
                if step == 0:
                    start(f_copy(e, far, d))
                start(d_copy(e, far, FROM_LEFT if d == 0 else FROM_RIGHT, h))

    def take_far(e, far):
        for d in range(2):
            f_copy(e, far, d).wait_recv()
            start(d_copy(e, far, FAR, d))

    def wait_core(e, far, positions):
        for pos in positions:
            for h in range(2):
                d_copy(e, far, pos, h).wait_recv()

    def multiply(e, lo, hi):
        first, last = lo == 0, hi == 8
        k = (hi - lo) * 128
        right = gr[e, 2 * lo:2 * hi].reshape(k, 256)

        def body(j, state):
            total, most = state
            cols = pl.ds(pl.multiple_of(j * TILE, TILE), TILE)
            left = buf[e, 4 * lo:4 * hi, :, cols].reshape(k, TILE)
            part = lax.dot_general(left, right, (((0,), (0,)), ((), ())), preferred_element_type=F32)
            if not first:
                part = part + prod[e, cols, :]
            prod[e, cols, :] = part
            if last:
                total = total + jnp.sum((part * part).reshape(TILE // 8, 8, 256), axis=0)
                most = jnp.maximum(most, jnp.max(jnp.abs(part).reshape(TILE // 8, 8, 256), axis=0))
            return total, most

        none = jnp.zeros((8, 256), F32)
        total, most = lax.fori_loop(0, 3584 // TILE, body, (none, none))
        if last:
            sq[e] = total
            top[e] = most
            for i, to in tp_peers:
                start(remote(sq.at[e], sq_in.at[e, i], n_s.at[e, i], n_r.at[e, i], to))

    def begins(d, r):
        return 4 if (r in (1, 3)) == (d == 0) else 3

    def block(e, row_y, r):
        rows = pl.ds(pl.multiple_of((row_y * 4 + lax.rem(zl + r, 4)) * ROWS, 16), ROWS)
        return prod[e, rows, :]

    def ahead(d, dist):
        return lax.rem(y + (dist if d == 0 else 8 - dist), 8)

    def tile_max(value):
        return jnp.broadcast_to(jnp.max(value, axis=(0, 1), keepdims=True), (8, 256))

    order = [(0, 1), (1, 2), (0, 3), (1, 0), (1, 1), (0, 2), (1, 3), (0, 0)]

    def s_copy(e, d, r):
        return remote(sout.at[e, d, r], sin.at[e, d, r], s_s.at[e, d, r], s_r.at[e, d, r], y_next[d])

    def w_copy(e, r):
        return remote(zout.at[e, r], zin.at[e, r], w_s.at[e, r], w_r.at[e, r], line(r))

    def first_hop(e):
        most = tile_max(top[e]) * 1.0001 + 1e-35
        for d, r in order:
            sout[e, d, r] = encode(block(e, ahead(d, begins(d, r)), r), most)
            start(s_copy(e, d, r))
        for r in range(1, 4):
            zout[e, r] = encode(block(e, y, r), most)
            start(w_copy(e, r))
        return most

    def factor(e):
        total = sq[e]
        for i, to in tp_peers:
            remote(sq.at[e], sq_in.at[e, i], n_s.at[e, i], n_r.at[e, i], to).wait_recv()
            total = total + sq_in[e, i]
        norm = jnp.sqrt(jnp.broadcast_to(jnp.sum(total, axis=(0, 1), keepdims=True), (8, 256)))
        return jnp.minimum(1.0, clip[0] / (norm + 1e-06))

    def b_copy(e, k):
        return remote(bound.at[e], bound_in.at[e, k], b_s.at[e, k], b_r.at[e, k], peer(dy=k))

    def send_bound(e, value):
        bound[e] = value
        for k in (1, 7, 2, 6, 3, 5, 4):
            start(b_copy(e, k))

    pass_relay(0)
    take_x(0, 0)
    take_x(1, 0)
    take_z(0)
    start(z_copy(1, 0, 0))
    start(z_copy(1, 1, 0))
    wait_core(0, 0, [OWN, FROM_RIGHT, FROM_LEFT])
    multiply(0, 0, 3)
    pass_relay(1)
    wait_core(1, 0, [OWN, FROM_RIGHT, FROM_LEFT])
    multiply(1, 0, 3)
    take_far(0, 0)
    take_far(1, 0)
    take_x(0, 1)
    take_z(1)
    wait_core(0, 0, [FAR])
    wait_core(0, 1, [OWN, FROM_RIGHT, FROM_LEFT])
    multiply(0, 3, 7)
    take_far(0, 1)
    wait_core(0, 1, [FAR])
    multiply(0, 7, 8)
    wait_core(1, 0, [FAR])
    wait_core(1, 1, [OWN])
    multiply(1, 3, 5)
    take_x(1, 1)
    most0 = first_hop(0)
    wait_core(1, 1, [FROM_RIGHT, FROM_LEFT])
    multiply(1, 5, 7)
    factor0 = factor(0)
    bound0 = factor0 * most0
    send_bound(0, bound0)
    take_far(1, 1)
    wait_core(1, 1, [FAR])
    multiply(1, 7, 8)
    most1 = first_hop(1)
    factor1 = factor(1)
    bound1 = factor1 * most1
    send_bound(1, bound1)
    mine = bound0 + bound1

    def own(row_y, r):
        terms = [
            scale[None] * block(e, row_y, r).reshape(ROWS // 8, 8, 256)
            for e, scale in enumerate((factor0, factor1))
        ]
        return (terms[0] + terms[1]).reshape(ROWS, 256)

    def v_copy(r):
        return remote(bound, line_bound.at[r], v_s.at[r], v_r.at[r], line(r))

    for r in range(1, 4):
        start(v_copy(r))

    def t_copy(d, r):
        return remote(
            limit_out.at[d, begins(d, r) - 3], limit_in.at[d, r], t_s.at[d, r], t_r.at[d, r],
            line(r, 1 if d == 0 else 7),
        )

    def y_copy(d, dist, r):
        return remote(
            yout.at[d, dist - 1, r], yin.at[d, dist - 1, r],
            y_s.at[d, dist - 1, r], y_r.at[d, dist - 1, r],
            y_next[d] if dist > 1 else line(r, 1 if d == 0 else 7),
        )

    bounds, sums = {}, {}

    def near(k):
        if k not in bounds:
            for e in range(2):
                b_copy(e, k).wait_recv()
            bounds[k] = bound_in[0, k] + bound_in[1, k]
        return bounds[k]

    def near_sum(d, n):
        if (d, n) not in sums:
            value = near(n if d == 0 else 8 - n)
            sums[d, n] = value if n == 1 else near_sum(d, n - 1) + value
        return sums[d, n]

    def arrived(d, dist, r):
        steps = begins(d, r) - dist
        if steps > 1:
            y_copy(d, dist + 1, r).wait_recv()
            return decode(yin[d, dist, r], near_sum(d, steps))
        value = 0.0
        for e in range(2):
            s_copy(e, d, r).wait_recv()
            value = value + decode(sin[e, d, r], bound_in[e, 1 if d == 0 else 7])
        return value

    def pass_on(steps, d, r):
        dist = begins(d, r) - steps
        limit = mine + near_sum(d, steps)
        value = own(ahead(d, dist), r) + arrived(d, dist, r)
        yout[d, dist - 1, r] = encode(value, limit)
        start(y_copy(d, dist, r))

    for d, r in order:
        pass_on(1, d, r)
    for d in range(2):
        for k in range(2):
            limit_out[d, k] = mine + near_sum(d, k + 2)
    for r in range(1, 4):
        for d in range(2):
            start(t_copy(d, r))
    for steps in (2, 3):
        for d, r in order:
            if begins(d, r) > steps:
                pass_on(steps, d, r)

    result = own(y, 0)
    for r in range(1, 4):
        v_copy(r).wait_recv()
        for e in range(2):
            w_copy(e, r).wait_recv()
            result = result + decode(zin[e, r], line_bound[r, e])
    settle(len(started) - 12)
    for d, r in order[4:] + order[:4]:
        if r == 0:
            result = result + arrived(d, 0, 0)
        else:
            t_copy(d, r).wait_recv()
            y_copy(d, 1, r).wait_recv()
            result = result + decode(yin[d, 0, r], limit_in[d, r])
    out[...] = result
    settle(len(started))


def body(activations, out_grads, clip_bound):
    vmem, dma = pltpu.VMEM, pltpu.SemaphoreType.DMA
    return pl.pallas_call(
        kernel,
        out_shape=jax.ShapeDtypeStruct((ROWS, 256), F32),
        in_specs=[
            pl.BlockSpec(memory_space=pl.ANY),
            pl.BlockSpec(memory_space=pl.ANY),
            pl.BlockSpec(memory_space=pltpu.SMEM),
        ],
        out_specs=pl.BlockSpec(memory_space=pltpu.VMEM),
        scratch_shapes=[
            vmem((2, 1024, 256), jnp.bfloat16),
            vmem((2, 32, HALF, 3584), jnp.bfloat16),
            vmem((2, 2, HALF, 3584), jnp.bfloat16),
            vmem((2, 16, 64, 256), jnp.bfloat16),
            vmem((2, 3584, 256), F32),
            vmem((2, 8, 256), F32),
            vmem((2, 16, 8, 256), F32),
            vmem((2, 8, 256), F32),
            vmem((2, 8, 256), F32),
            vmem((2, 8, 8, 256), F32),
            vmem((4, 2, 8, 256), F32),
            vmem((2, 2, 8, 256), F32),
            vmem((2, 4, 8, 256), F32),
            vmem((2, 2, 4, ROWS, 256), jnp.bfloat16),
            vmem((2, 2, 4, ROWS, 256), jnp.bfloat16),
            vmem((2, 3, 4, ROWS, 256), jnp.bfloat16),
            vmem((2, 3, 4, ROWS, 256), jnp.bfloat16),
            vmem((2, 4, ROWS, 256), jnp.bfloat16),
            vmem((2, 4, ROWS, 256), jnp.bfloat16),
            dma((2, 2)),
            dma,
            dma((2, 2, 2, 2)), dma((2, 2, 2, 2)),
            dma((2, 2, 2)), dma((2, 2, 2)),
            dma((2, 2, 2)), dma((2, 2, 2)),
            dma((2, 2, 4, 2)), dma((2, 2, 4, 2)),
            dma((2, 16)), dma((2, 16)),
            dma((2, 8)), dma((2, 8)),
            dma((4,)), dma((4,)),
            dma((2, 4)), dma((2, 4)),
            dma((2, 2, 4)), dma((2, 2, 4)),
            dma((2, 3, 4)), dma((2, 3, 4)),
            dma((2, 4)), dma((2, 4)),
        ],
        compiler_params=pltpu.CompilerParams(
            collective_id=0, has_side_effects=True, vmem_limit_bytes=56 * 2**20
        ),
        cost_estimate=pl.CostEstimate(flops=3758096384, bytes_accessed=20000000, transcendentals=1000000),
    )(activations, out_grads, clip_bound)


def solution(mesh):
    return jax.shard_map(
        body,
        mesh=mesh,
        in_specs=(P("dp", "tp", None), P("dp", None, "tp"), P()),
        out_specs=P("dp", "tp"),
        check_vma=False,
    )
```

```python
import math

import jax
import jax.numpy as jnp
from jax import lax
from jax.experimental import pallas as pl
from jax.experimental.pallas import tpu as pltpu
from jax.sharding import PartitionSpec as P

MESH = pl.DeviceIdType.MESH
F32 = jnp.float32
NX, NY, NZL, NZH = 4, 8, 4, 2
HALF, PIECE = 32, 16
ROWS = 112
TILE = 512
POWER, SHIFT = 11, 120
OFFSET = (0, 1, 3, 2)
OWN, FROM_RIGHT, FROM_LEFT, FAR = 0, 1, 2, 3


def encode(value, bound):
    u = (value.reshape(-1, 8, 256) * (2.0 ** (SHIFT / POWER) / bound)[None]).reshape(value.shape)
    u2 = u * u
    u4 = u2 * u2
    return ((u4 * u4) * (u2 * u)).astype(jnp.bfloat16)


def decode(code, bound):
    code = code.astype(F32)
    size = jnp.exp2(jnp.log(jnp.maximum(jnp.abs(code), 2.0**-126)) * (1.0 / (POWER * math.log(2.0))))
    size = (size.reshape(-1, 8, 256) * (2.0 ** (-SHIFT / POWER) * bound)[None]).reshape(code.shape)
    return jnp.where(code < 0, -size, size)


def kernel(
    act, grads_in, clip, out,
    grads, buf, relay, gr, prod, sq, sq_in, top, bound, bound_in, line_bound, limit_out, limit_in, sout, sin, yout, yin, zout, zin,
    load_sem, grads_sem, x_s, x_r, f_s, f_r, z_s, z_r, d_s, d_r, n_s, n_r, b_s, b_r, v_s, v_r, t_s, t_r, s_s, s_r, y_s, y_r, w_s, w_r,
):
    dp, tp = lax.axis_index("dp"), lax.axis_index("tp")
    y, zl = lax.div(dp, 4), lax.rem(dp, 4)
    zh, x, c = lax.div(tp, 8), lax.rem(lax.div(tp, 2), 4), lax.rem(tp, 2)
    z = zh * 4 + zl

    def peer(dx=0, dy=0, dz=0, dc=0):
        nz = lax.rem(z + dz, 8)
        return (
            lax.rem(y + dy, 8) * 4 + lax.rem(nz, 4),
            lax.div(nz, 4) * 8 + lax.rem(x + dx, 4) * 2 + lax.rem(c + dc, 2),
        )

    def line(r, dy=0):
        return (lax.rem(y + dy, 8) * 4 + lax.rem(zl + r, 4), tp)

    tp_peers = [(i, peer(dx=(i // 2) % 4, dz=4 * (i // 8), dc=i % 2)) for i in range(15, 0, -1)]
    z_far = {0: peer(dz=2), 1: peer(dz=6)}
    x_next = {0: peer(dx=1), 1: peer(dx=3)}
    y_next = {0: peer(dy=1), 1: peer(dy=7)}
    other = peer(dc=1)

    def unit(e, far, pos, core, h):
        return buf.at[e, 16 * far + 4 * pos + 2 * core + h]

    def remote(src, dst, s, r, to):
        return pltpu.make_async_remote_copy(
            src_ref=src, dst_ref=dst, send_sem=s, recv_sem=r, device_id=to, device_id_type=MESH
        )

    started = []

    def settle(count):
        for copy in started[:count]:
            copy.wait_send()
        del started[:count]

    def start(copy):
        copy.start()
        started.append(copy)

    def piece(block, t):
        return block if t is None else block.at[pl.ds(PIECE * t, PIECE)]

    def x_copy(e, far, d, h, t=None):
        return remote(
            piece(unit(e, far, OWN, 0, h), t),
            piece(unit(e, far, FROM_LEFT if d == 0 else FROM_RIGHT, 0, h), t),
            x_s.at[e, far, d, h, t or 0], x_r.at[e, far, d, h, t or 0], x_next[d],
        )

    def f_copy(e, far, d, t=None):
        return remote(
            piece(unit(e, far, FROM_LEFT if d == 0 else FROM_RIGHT, 0, d), t),
            piece(unit(e, far, FAR, 0, d), t),
            f_s.at[e, far, d, t or 0], f_r.at[e, far, d, t or 0], x_next[d],
        )

    def z_copy(e, d, leg, t):
        src = piece(unit(e, 0, OWN, 0, d), t) if leg == 0 else relay.at[e, d, t]
        dst = relay.at[e, d, t] if leg == 0 else piece(unit(e, 1, OWN, 0, d), t)
        return remote(src, dst, z_s.at[e, d, leg, t], z_r.at[e, d, leg, t], z_far[d])

    def d_copy(e, far, pos, h, t=None):
        return remote(
            piece(unit(e, far, pos, 0, h), t), piece(unit(e, far, pos, 1, h), t),
            d_s.at[e, far, pos, h, t or 0], d_r.at[e, far, pos, h, t or 0], other,
        )

    loads = {
        (e, h): pltpu.make_async_copy(
            act.at[e, pl.ds(h * HALF, HALF)], unit(e, 0, OWN, 0, h), load_sem.at[e, h]
        )
        for e in range(2) for h in range(2)
    }
    for load in loads.values():
        load.start()
    grads_load = pltpu.make_async_copy(grads_in, grads, grads_sem)
    grads_load.start()

    def send_z(e, t):
        for d in range(2):
            start(z_copy(e, d, 0, t))

    barrier = pltpu.get_barrier_semaphore()
    greeted = [to for _, to in tp_peers] + list(z_far.values())
    greeted += [peer(dy=k) for k in range(1, 8)]
    greeted += [line(r, dy) for r in range(1, 4) for dy in (0, 1, 7)]
    for to in greeted:
        pl.semaphore_signal(barrier, inc=1, device_id=to, device_id_type=MESH)
    pl.semaphore_wait(barrier, len(greeted))

    for e in range(2):
        for h in range(2):
            loads[e, h].wait()
        if e == 0:
            send_z(0, 0)
        for h in range(2):
            for d in range(2):
                start(x_copy(e, 0, d, h if d == 0 else 1 - h))
        for h in range(2):
            start(d_copy(e, 0, OWN, h))

    grads_load.wait()
    for e in range(2):
        for far in range(2):
            for pos in range(4):
                for core in range(2):
                    block = (
                        lax.rem(zh + far, 2) * 8 + lax.rem(x + OFFSET[pos], 4) * 2 + lax.rem(c + core, 2)
                    )
                    rows = pl.ds(pl.multiple_of(block * 64, 64), 64)
                    gr[e, 8 * far + 2 * pos + core] = grads[e, rows, :]

    def pass_relay(e, t):
        for d in range(2):
            z_copy(e, d, 0, t).wait_recv()
            start(z_copy(e, d, 1, t))

    def take_z(e, t):
        for d in range(2):
            z_copy(e, d, 1, t).wait_recv()
            for k in range(2):
                start(x_copy(e, 1, k, d, t))
            start(d_copy(e, 1, OWN, d, t))

    def take_x(e, far, t=None):
        for step in range(2):
            for d in range(2):
                h = d if step == 0 else 1 - d
                x_copy(e, far, d, h, t).wait_recv()
                if step == 0:
                    start(f_copy(e, far, d, t))
                start(d_copy(e, far, FROM_LEFT if d == 0 else FROM_RIGHT, h, t))

    def take_far(e, far, t=None):
        for d in range(2):
            f_copy(e, far, d, t).wait_recv()
            start(d_copy(e, far, FAR, d, t))

    def wait_core(e, far, positions):
        for pos in positions:
            for h in range(2):
                for t in (0, 1) if far else (None,):
                    d_copy(e, far, pos, h, t).wait_recv()

    def multiply(e, lo, hi):
        first, last = lo == 0, hi == 8
        k = (hi - lo) * 128
        right = gr[e, 2 * lo:2 * hi].reshape(k, 256)

        def body(j, state):
            total, most = state
            cols = pl.ds(pl.multiple_of(j * TILE, TILE), TILE)
            left = buf[e, 4 * lo:4 * hi, :, cols].reshape(k, TILE)
            part = lax.dot_general(left, right, (((0,), (0,)), ((), ())), preferred_element_type=F32)
            if not first:
                part = part + prod[e, cols, :]
            prod[e, cols, :] = part
            if last:
                total = total + jnp.sum((part * part).reshape(TILE // 8, 8, 256), axis=0)
                most = jnp.maximum(most, jnp.max(jnp.abs(part).reshape(TILE // 8, 8, 256), axis=0))
            return total, most

        none = jnp.zeros((8, 256), F32)
        total, most = lax.fori_loop(0, 3584 // TILE, body, (none, none))
        if last:
            sq[e] = total
            top[e] = most
            for i, to in tp_peers:
                start(remote(sq.at[e], sq_in.at[e, i], n_s.at[e, i], n_r.at[e, i], to))

    def begins(d, r):
        return 4 if (r in (1, 3)) == (d == 0) else 3

    def block(e, row_y, r):
        rows = pl.ds(pl.multiple_of((row_y * 4 + lax.rem(zl + r, 4)) * ROWS, 16), ROWS)
        return prod[e, rows, :]

    def ahead(d, dist):
        return lax.rem(y + (dist if d == 0 else 8 - dist), 8)

    def tile_max(value):
        return jnp.broadcast_to(jnp.max(value, axis=(0, 1), keepdims=True), (8, 256))

    order = [(0, 1), (1, 2), (0, 3), (1, 0), (1, 1), (0, 2), (1, 3), (0, 0)]

    def s_copy(e, d, r):
        return remote(sout.at[e, d, r], sin.at[e, d, r], s_s.at[e, d, r], s_r.at[e, d, r], y_next[d])

    def w_copy(e, r):
        return remote(zout.at[e, r], zin.at[e, r], w_s.at[e, r], w_r.at[e, r], line(r))

    def first_hop(e):
        most = tile_max(top[e]) * 1.0001 + 1e-35
        for d, r in order:
            sout[e, d, r] = encode(block(e, ahead(d, begins(d, r)), r), most)
            start(s_copy(e, d, r))
        for r in range(1, 4):
            zout[e, r] = encode(block(e, y, r), most)
            start(w_copy(e, r))
        return most

    def factor(e):
        total = sq[e]
        for i, to in tp_peers:
            remote(sq.at[e], sq_in.at[e, i], n_s.at[e, i], n_r.at[e, i], to).wait_recv()
            total = total + sq_in[e, i]
        norm = jnp.sqrt(jnp.broadcast_to(jnp.sum(total, axis=(0, 1), keepdims=True), (8, 256)))
        return jnp.minimum(1.0, clip[0] / (norm + 1e-06))

    def b_copy(e, k):
        return remote(bound.at[e], bound_in.at[e, k], b_s.at[e, k], b_r.at[e, k], peer(dy=k))

    def send_bound(e, value):
        bound[e] = value
        for k in (1, 7, 2, 6, 3, 5, 4):
            start(b_copy(e, k))

    pass_relay(0, 0)
    send_z(0, 1)
    take_x(0, 0)
    take_x(1, 0)
    pass_relay(0, 1)
    take_z(0, 0)
    send_z(1, 0)
    wait_core(0, 0, [OWN, FROM_RIGHT, FROM_LEFT])
    multiply(0, 0, 3)
    pass_relay(1, 0)
    take_z(0, 1)
    send_z(1, 1)
    wait_core(1, 0, [OWN, FROM_RIGHT, FROM_LEFT])
    multiply(1, 0, 3)
    take_far(0, 0)
    take_far(1, 0)
    take_x(0, 1, 0)
    pass_relay(1, 1)
    take_z(1, 0)
    take_x(0, 1, 1)
    wait_core(0, 0, [FAR])
    wait_core(0, 1, [OWN, FROM_RIGHT, FROM_LEFT])
    multiply(0, 3, 7)
    take_z(1, 1)
    take_far(0, 1, 0)
    take_far(0, 1, 1)
    wait_core(0, 1, [FAR])
    multiply(0, 7, 8)
    take_x(1, 1, 0)
    wait_core(1, 0, [FAR])
    wait_core(1, 1, [OWN])
    multiply(1, 3, 5)
    take_x(1, 1, 1)
    most0 = first_hop(0)
    wait_core(1, 1, [FROM_RIGHT, FROM_LEFT])
    multiply(1, 5, 7)
    factor0 = factor(0)
    bound0 = factor0 * most0
    send_bound(0, bound0)
    take_far(1, 1, 0)
    take_far(1, 1, 1)
    wait_core(1, 1, [FAR])
    multiply(1, 7, 8)
    most1 = first_hop(1)
    factor1 = factor(1)
    bound1 = factor1 * most1
    send_bound(1, bound1)
    mine = bound0 + bound1

    def own(row_y, r):
        terms = [
            scale[None] * block(e, row_y, r).reshape(ROWS // 8, 8, 256)
            for e, scale in enumerate((factor0, factor1))
        ]
        return (terms[0] + terms[1]).reshape(ROWS, 256)

    def v_copy(r):
        return remote(bound, line_bound.at[r], v_s.at[r], v_r.at[r], line(r))

    for r in range(1, 4):
        start(v_copy(r))

    def t_copy(d, r):
        return remote(
            limit_out.at[d, begins(d, r) - 3], limit_in.at[d, r], t_s.at[d, r], t_r.at[d, r],
            line(r, 1 if d == 0 else 7),
        )

    def y_copy(d, dist, r):
        return remote(
            yout.at[d, dist - 1, r], yin.at[d, dist - 1, r],
            y_s.at[d, dist - 1, r], y_r.at[d, dist - 1, r],
            y_next[d] if dist > 1 else line(r, 1 if d == 0 else 7),
        )

    bounds, sums = {}, {}

    def near(k):
        if k not in bounds:
            for e in range(2):
                b_copy(e, k).wait_recv()
            bounds[k] = bound_in[0, k] + bound_in[1, k]
        return bounds[k]

    def near_sum(d, n):
        if (d, n) not in sums:
            value = near(n if d == 0 else 8 - n)
            sums[d, n] = value if n == 1 else near_sum(d, n - 1) + value
        return sums[d, n]

    def arrived(d, dist, r):
        steps = begins(d, r) - dist
        if steps > 1:
            y_copy(d, dist + 1, r).wait_recv()
            return decode(yin[d, dist, r], near_sum(d, steps))
        value = 0.0
        for e in range(2):
            s_copy(e, d, r).wait_recv()
            value = value + decode(sin[e, d, r], bound_in[e, 1 if d == 0 else 7])
        return value

    def pass_on(steps, d, r):
        dist = begins(d, r) - steps
        limit = mine + near_sum(d, steps)
        value = own(ahead(d, dist), r) + arrived(d, dist, r)
        yout[d, dist - 1, r] = encode(value, limit)
        start(y_copy(d, dist, r))

    for d, r in order:
        pass_on(1, d, r)
    for d in range(2):
        for k in range(2):
            limit_out[d, k] = mine + near_sum(d, k + 2)
    for r in range(1, 4):
        for d in range(2):
            start(t_copy(d, r))
    for steps in (2, 3):
        for d, r in order:
            if begins(d, r) > steps:
                pass_on(steps, d, r)

    result = own(y, 0)
    for r in range(1, 4):
        v_copy(r).wait_recv()
        for e in range(2):
            w_copy(e, r).wait_recv()
            result = result + decode(zin[e, r], line_bound[r, e])
    settle(len(started) - 12)
    for d, r in order[4:] + order[:4]:
        if r == 0:
            result = result + arrived(d, 0, 0)
        else:
            t_copy(d, r).wait_recv()
            y_copy(d, 1, r).wait_recv()
            result = result + decode(yin[d, 0, r], limit_in[d, r])
    out[...] = result
    settle(len(started))


def body(activations, out_grads, clip_bound):
    vmem, dma = pltpu.VMEM, pltpu.SemaphoreType.DMA
    return pl.pallas_call(
        kernel,
        out_shape=jax.ShapeDtypeStruct((ROWS, 256), F32),
        in_specs=[
            pl.BlockSpec(memory_space=pl.ANY),
            pl.BlockSpec(memory_space=pl.ANY),
            pl.BlockSpec(memory_space=pltpu.SMEM),
        ],
        out_specs=pl.BlockSpec(memory_space=pltpu.VMEM),
        scratch_shapes=[
            vmem((2, 1024, 256), jnp.bfloat16),
            vmem((2, 32, HALF, 3584), jnp.bfloat16),
            vmem((2, 2, 2, PIECE, 3584), jnp.bfloat16),
            vmem((2, 16, 64, 256), jnp.bfloat16),
            vmem((2, 3584, 256), F32),
            vmem((2, 8, 256), F32),
            vmem((2, 16, 8, 256), F32),
            vmem((2, 8, 256), F32),
            vmem((2, 8, 256), F32),
            vmem((2, 8, 8, 256), F32),
            vmem((4, 2, 8, 256), F32),
            vmem((2, 2, 8, 256), F32),
            vmem((2, 4, 8, 256), F32),
            vmem((2, 2, 4, ROWS, 256), jnp.bfloat16),
            vmem((2, 2, 4, ROWS, 256), jnp.bfloat16),
            vmem((2, 3, 4, ROWS, 256), jnp.bfloat16),
            vmem((2, 3, 4, ROWS, 256), jnp.bfloat16),
            vmem((2, 4, ROWS, 256), jnp.bfloat16),
            vmem((2, 4, ROWS, 256), jnp.bfloat16),
            dma((2, 2)),
            dma,
            dma((2, 2, 2, 2, 2)), dma((2, 2, 2, 2, 2)),
            dma((2, 2, 2, 2)), dma((2, 2, 2, 2)),
            dma((2, 2, 2, 2)), dma((2, 2, 2, 2)),
            dma((2, 2, 4, 2, 2)), dma((2, 2, 4, 2, 2)),
            dma((2, 16)), dma((2, 16)),
            dma((2, 8)), dma((2, 8)),
            dma((4,)), dma((4,)),
            dma((2, 4)), dma((2, 4)),
            dma((2, 2, 4)), dma((2, 2, 4)),
            dma((2, 3, 4)), dma((2, 3, 4)),
            dma((2, 4)), dma((2, 4)),
        ],
        compiler_params=pltpu.CompilerParams(
            collective_id=0, has_side_effects=True, vmem_limit_bytes=56 * 2**20
        ),
        cost_estimate=pl.CostEstimate(flops=3758096384, bytes_accessed=20000000, transcendentals=1000000),
    )(activations, out_grads, clip_bound)


def solution(mesh):
    return jax.shard_map(
        body,
        mesh=mesh,
        in_specs=(P("dp", "tp", None), P("dp", None, "tp"), P()),
        out_specs=P("dp", "tp"),
        check_vma=False,
    )
```

```python
import math

import jax
import jax.numpy as jnp
from jax import lax
from jax.experimental import pallas as pl
from jax.experimental.pallas import tpu as pltpu
from jax.sharding import PartitionSpec as P

MESH = pl.DeviceIdType.MESH
F32 = jnp.float32
NX, NY, NZL, NZH = 4, 8, 4, 2
HALF = 32
ROWS = 112
TILE = 512
POWER, SHIFT = 11, 120
OFFSET = (0, 1, 3, 2)
OWN, FROM_RIGHT, FROM_LEFT, FAR = 0, 1, 2, 3


def encode(value, bound):
    u = (value.reshape(-1, 8, 256) * (2.0 ** (SHIFT / POWER) / bound)[None]).reshape(value.shape)
    u2 = u * u
    u4 = u2 * u2
    return ((u4 * u4) * (u2 * u)).astype(jnp.bfloat16)


def decode(code, bound):
    code = code.astype(F32)
    size = jnp.exp2(jnp.log(jnp.maximum(jnp.abs(code), 2.0**-126)) * (1.0 / (POWER * math.log(2.0))))
    size = (size.reshape(-1, 8, 256) * (2.0 ** (-SHIFT / POWER) * bound)[None]).reshape(code.shape)
    return jnp.where(code < 0, -size, size)


def kernel(
    act, grads_in, clip, out,
    grads, buf, relay, gr, prod, sq, sq_in, top, bound, bound_in, line_bound, limit_out, limit_in, sout, sin, yout, yin, zout, zin,
    load_sem, grads_sem, x_s, x_r, f_s, f_r, z_s, z_r, d_s, d_r, n_s, n_r, b_s, b_r, v_s, v_r, t_s, t_r, s_s, s_r, y_s, y_r, w_s, w_r,
):
    dp, tp = lax.axis_index("dp"), lax.axis_index("tp")
    y, zl = lax.div(dp, 4), lax.rem(dp, 4)
    zh, x, c = lax.div(tp, 8), lax.rem(lax.div(tp, 2), 4), lax.rem(tp, 2)
    z = zh * 4 + zl

    def peer(dx=0, dy=0, dz=0, dc=0):
        nz = lax.rem(z + dz, 8)
        return (
            lax.rem(y + dy, 8) * 4 + lax.rem(nz, 4),
            lax.div(nz, 4) * 8 + lax.rem(x + dx, 4) * 2 + lax.rem(c + dc, 2),
        )

    def line(r, dy=0):
        return (lax.rem(y + dy, 8) * 4 + lax.rem(zl + r, 4), tp)

    square = [peer(dc=1), peer(dz=4), peer(dc=1, dz=4)]
    row = [peer(dx=k) for k in range(1, 4)]
    z_far = {0: peer(dz=2), 1: peer(dz=6)}
    x_next = {0: peer(dx=1), 1: peer(dx=3)}
    y_next = {0: peer(dy=1), 1: peer(dy=7)}
    other = peer(dc=1)

    def unit(e, far, pos, core, h):
        return buf.at[e, 16 * far + 4 * pos + 2 * core + h]

    def remote(src, dst, s, r, to):
        return pltpu.make_async_remote_copy(
            src_ref=src, dst_ref=dst, send_sem=s, recv_sem=r, device_id=to, device_id_type=MESH
        )

    started = []

    def settle(count):
        for copy in started[:count]:
            copy.wait_send()
        del started[:count]

    def start(copy):
        copy.start()
        started.append(copy)

    def x_copy(e, far, d, h):
        return remote(
            unit(e, far, OWN, 0, h), unit(e, far, FROM_LEFT if d == 0 else FROM_RIGHT, 0, h),
            x_s.at[e, far, d, h], x_r.at[e, far, d, h], x_next[d],
        )

    def f_copy(e, far, d):
        return remote(
            unit(e, far, FROM_LEFT if d == 0 else FROM_RIGHT, 0, d), unit(e, far, FAR, 0, d),
            f_s.at[e, far, d], f_r.at[e, far, d], x_next[d],
        )

    def z_copy(e, d, leg):
        src = unit(e, 0, OWN, 0, d) if leg == 0 else relay.at[e, d]
        dst = relay.at[e, d] if leg == 0 else unit(e, 1, OWN, 0, d)
        return remote(src, dst, z_s.at[e, d, leg], z_r.at[e, d, leg], z_far[d])

    def d_copy(e, far, pos, h):
        return remote(
            unit(e, far, pos, 0, h), unit(e, far, pos, 1, h),
            d_s.at[e, far, pos, h], d_r.at[e, far, pos, h], other,
        )

    loads = {
        (e, h): pltpu.make_async_copy(
            act.at[e, pl.ds(h * HALF, HALF)], unit(e, 0, OWN, 0, h), load_sem.at[e, h]
        )
        for e in range(2) for h in range(2)
    }
    for load in loads.values():
        load.start()
    grads_load = pltpu.make_async_copy(grads_in, grads, grads_sem)
    grads_load.start()

    barrier = pltpu.get_barrier_semaphore()
    greeted = square + row + list(z_far.values())
    greeted += [peer(dy=k) for k in range(1, 8)]
    greeted += [line(r, dy) for r in range(1, 4) for dy in (0, 1, 7)]
    for to in greeted:
        pl.semaphore_signal(barrier, inc=1, device_id=to, device_id_type=MESH)
    pl.semaphore_wait(barrier, len(greeted))

    for e in range(2):
        for h in range(2):
            loads[e, h].wait()
        if e == 0:
            start(z_copy(0, 0, 0))
            start(z_copy(0, 1, 0))
        for h in range(2):
            for d in range(2):
                start(x_copy(e, 0, d, h if d == 0 else 1 - h))
        for h in range(2):
            start(d_copy(e, 0, OWN, h))

    grads_load.wait()
    for e in range(2):
        for far in range(2):
            for pos in range(4):
                for core in range(2):
                    block = (
                        lax.rem(zh + far, 2) * 8 + lax.rem(x + OFFSET[pos], 4) * 2 + lax.rem(c + core, 2)
                    )
                    rows = pl.ds(pl.multiple_of(block * 64, 64), 64)
                    gr[e, 8 * far + 2 * pos + core] = grads[e, rows, :]

    def pass_relay(e):
        for d in range(2):
            z_copy(e, d, 0).wait_recv()
            start(z_copy(e, d, 1))

    def take_z(e):
        for d in range(2):
            z_copy(e, d, 1).wait_recv()
            for k in range(2):
                start(x_copy(e, 1, k, d))
            start(d_copy(e, 1, OWN, d))

    def take_x(e, far):
        for step in range(2):
            for d in range(2):
                h = d if step == 0 else 1 - d
                x_copy(e, far, d, h).wait_recv()
                if step == 0:
                    start(f_copy(e, far, d))
                start(d_copy(e, far, FROM_LEFT if d == 0 else FROM_RIGHT, h))

    def take_far(e, far):
        for d in range(2):
            f_copy(e, far, d).wait_recv()
            start(d_copy(e, far, FAR, d))

    def wait_core(e, far, positions):
        for pos in positions:
            for h in range(2):
                d_copy(e, far, pos, h).wait_recv()

    def norm_copies(e, stage):
        return [
            remote(sq.at[e, stage], sq_in.at[e, stage, i], n_s.at[e, stage, i], n_r.at[e, stage, i], to)
            for i, to in enumerate((square, row)[stage])
        ]

    def multiply(e, lo, hi):
        first, last = lo == 0, hi == 8
        k = (hi - lo) * 128
        right = gr[e, 2 * lo:2 * hi].reshape(k, 256)

        def body(j, state):
            total, most = state
            cols = pl.ds(pl.multiple_of(j * TILE, TILE), TILE)
            left = buf[e, 4 * lo:4 * hi, :, cols].reshape(k, TILE)
            part = lax.dot_general(left, right, (((0,), (0,)), ((), ())), preferred_element_type=F32)
            if not first:
                part = part + prod[e, cols, :]
            prod[e, cols, :] = part
            if last:
                total = total + jnp.sum((part * part).reshape(TILE // 8, 8, 256), axis=0)
                most = jnp.maximum(most, jnp.max(jnp.abs(part).reshape(TILE // 8, 8, 256), axis=0))
            return total, most

        none = jnp.zeros((8, 256), F32)
        total, most = lax.fori_loop(0, 3584 // TILE, body, (none, none))
        if last:
            sq[e, 0] = total
            for copy in norm_copies(e, 0):
                start(copy)
            top[e] = jnp.broadcast_to(jnp.max(most, axis=(0, 1), keepdims=True), (8, 256)) * 1.0001 + 1e-35

    def begins(d, r):
        return 4 if (r in (1, 3)) == (d == 0) else 3

    def block(e, row_y, r):
        rows = pl.ds(pl.multiple_of((row_y * 4 + lax.rem(zl + r, 4)) * ROWS, 16), ROWS)
        return prod[e, rows, :]

    def ahead(d, dist):
        return lax.rem(y + (dist if d == 0 else 8 - dist), 8)

    order = [(0, 1), (1, 2), (0, 3), (1, 0), (1, 1), (0, 2), (1, 3), (0, 0)]

    def s_copy(e, d, r):
        return remote(sout.at[e, d, r], sin.at[e, d, r], s_s.at[e, d, r], s_r.at[e, d, r], y_next[d])

    def w_copy(e, r):
        return remote(zout.at[e, r], zin.at[e, r], w_s.at[e, r], w_r.at[e, r], line(r))

    def first_hop(e, chains):
        limit = top[e]
        for d, r in chains:
            sout[e, d, r] = encode(block(e, ahead(d, begins(d, r)), r), limit)
            start(s_copy(e, d, r))

    def send_raw(e):
        limit = top[e]
        for r in range(1, 4):
            zout[e, r] = encode(block(e, y, r), limit)
            start(w_copy(e, r))

    def gathered(e, stage):
        total = sq[e, stage]
        for i, copy in enumerate(norm_copies(e, stage)):
            copy.wait_recv()
            total = total + sq_in[e, stage, i]
        return total

    def pass_norm(e):
        sq[e, 1] = gathered(e, 0)
        for copy in norm_copies(e, 1):
            start(copy)

    def factor(e):
        total = gathered(e, 1)
        norm = jnp.sqrt(jnp.broadcast_to(jnp.sum(total, axis=(0, 1), keepdims=True), (8, 256)))
        return jnp.minimum(1.0, clip[0] / (norm + 1e-06))

    def b_copy(k):
        return remote(bound, bound_in.at[k], b_s.at[k], b_r.at[k], peer(dy=k))

    pass_relay(0)
    take_x(0, 0)
    take_x(1, 0)
    take_z(0)
    start(z_copy(1, 0, 0))
    start(z_copy(1, 1, 0))
    wait_core(0, 0, [OWN, FROM_RIGHT, FROM_LEFT])
    multiply(0, 0, 3)
    pass_relay(1)
    wait_core(1, 0, [OWN, FROM_RIGHT, FROM_LEFT])
    multiply(1, 0, 3)
    take_far(0, 0)
    take_far(1, 0)
    take_x(0, 1)
    take_z(1)
    wait_core(0, 0, [FAR])
    wait_core(0, 1, [OWN, FROM_RIGHT, FROM_LEFT])
    multiply(0, 3, 7)
    take_far(0, 1)
    wait_core(0, 1, [FAR])
    multiply(0, 7, 8)
    wait_core(1, 0, [FAR])
    wait_core(1, 1, [OWN])
    multiply(1, 3, 5)
    take_x(1, 1)
    first_hop(0, order[:4])
    pass_norm(0)
    first_hop(0, order[4:])
    send_raw(0)
    wait_core(1, 1, [FROM_RIGHT, FROM_LEFT])
    multiply(1, 5, 7)
    take_far(1, 1)
    wait_core(1, 1, [FAR])
    multiply(1, 7, 8)
    first_hop(1, order[:4])
    pass_norm(1)
    first_hop(1, order[4:])
    factor0 = factor(0)
    factor1 = factor(1)
    bound[0] = factor0 * top[0]
    bound[1] = factor1 * top[1]
    for k in (1, 7, 2, 6, 3, 5, 4):
        start(b_copy(k))
    mine = bound[0] + bound[1]
    send_raw(1)

    def own(row_y, r):
        terms = [
            scale[None] * block(e, row_y, r).reshape(ROWS // 8, 8, 256)
            for e, scale in enumerate((factor0, factor1))
        ]
        return (terms[0] + terms[1]).reshape(ROWS, 256)

    def v_copy(r):
        return remote(bound, line_bound.at[r], v_s.at[r], v_r.at[r], line(r))

    def t_copy(d, r):
        return remote(
            limit_out.at[d, begins(d, r) - 3], limit_in.at[d, r], t_s.at[d, r], t_r.at[d, r],
            line(r, 1 if d == 0 else 7),
        )

    def y_copy(d, dist, r):
        return remote(
            yout.at[d, dist - 1, r], yin.at[d, dist - 1, r],
            y_s.at[d, dist - 1, r], y_r.at[d, dist - 1, r],
            y_next[d] if dist > 1 else line(r, 1 if d == 0 else 7),
        )

    bounds, sums = {}, {}

    def near(k):
        if k not in bounds:
            b_copy(k).wait_recv()
            bounds[k] = bound_in[k, 0] + bound_in[k, 1]
        return bounds[k]

    def near_sum(d, n):
        if (d, n) not in sums:
            value = near(n if d == 0 else 8 - n)
            sums[d, n] = value if n == 1 else near_sum(d, n - 1) + value
        return sums[d, n]

    def arrived(d, dist, r):
        steps = begins(d, r) - dist
        if steps > 1:
            y_copy(d, dist + 1, r).wait_recv()
            return decode(yin[d, dist, r], near_sum(d, steps))
        value = 0.0
        for e in range(2):
            s_copy(e, d, r).wait_recv()
            value = value + decode(sin[e, d, r], bound_in[1 if d == 0 else 7, e])
        return value

    def pass_on(steps, d, r):
        dist = begins(d, r) - steps
        limit = mine + near_sum(d, steps)
        value = own(ahead(d, dist), r) + arrived(d, dist, r)
        yout[d, dist - 1, r] = encode(value, limit)
        start(y_copy(d, dist, r))

    for d, r in order:
        pass_on(1, d, r)
    for d, r in order:
        if begins(d, r) > 2:
            pass_on(2, d, r)
    for d in range(2):
        for k in range(2):
            limit_out[d, k] = mine + near_sum(d, k + 2)
    for r in range(1, 4):
        start(v_copy(r))
        for d in range(2):
            start(t_copy(d, r))
    for d, r in order:
        if begins(d, r) > 3:
            pass_on(3, d, r)

    result = own(y, 0)
    for r in range(1, 4):
        v_copy(r).wait_recv()
        for e in range(2):
            w_copy(e, r).wait_recv()
            result = result + decode(zin[e, r], line_bound[r, e])
    settle(len(started) - 12)
    for d, r in order[4:] + order[:4]:
        if r == 0:
            result = result + arrived(d, 0, 0)
        else:
            t_copy(d, r).wait_recv()
            y_copy(d, 1, r).wait_recv()
            result = result + decode(yin[d, 0, r], limit_in[d, r])
    out[...] = result
    settle(len(started))


def body(activations, out_grads, clip_bound):
    vmem, dma = pltpu.VMEM, pltpu.SemaphoreType.DMA
    return pl.pallas_call(
        kernel,
        out_shape=jax.ShapeDtypeStruct((ROWS, 256), F32),
        in_specs=[
            pl.BlockSpec(memory_space=pl.ANY),
            pl.BlockSpec(memory_space=pl.ANY),
            pl.BlockSpec(memory_space=pltpu.SMEM),
        ],
        out_specs=pl.BlockSpec(memory_space=pltpu.VMEM),
        scratch_shapes=[
            vmem((2, 1024, 256), jnp.bfloat16),
            vmem((2, 32, HALF, 3584), jnp.bfloat16),
            vmem((2, 2, HALF, 3584), jnp.bfloat16),
            vmem((2, 16, 64, 256), jnp.bfloat16),
            vmem((2, 3584, 256), F32),
            vmem((2, 2, 8, 256), F32),
            vmem((2, 2, 3, 8, 256), F32),
            vmem((2, 8, 256), F32),
            vmem((2, 8, 256), F32),
            vmem((8, 2, 8, 256), F32),
            vmem((4, 2, 8, 256), F32),
            vmem((2, 2, 8, 256), F32),
            vmem((2, 4, 8, 256), F32),
            vmem((2, 2, 4, ROWS, 256), jnp.bfloat16),
            vmem((2, 2, 4, ROWS, 256), jnp.bfloat16),
            vmem((2, 3, 4, ROWS, 256), jnp.bfloat16),
            vmem((2, 3, 4, ROWS, 256), jnp.bfloat16),
            vmem((2, 4, ROWS, 256), jnp.bfloat16),
            vmem((2, 4, ROWS, 256), jnp.bfloat16),
            dma((2, 2)),
            dma,
            dma((2, 2, 2, 2)), dma((2, 2, 2, 2)),
            dma((2, 2, 2)), dma((2, 2, 2)),
            dma((2, 2, 2)), dma((2, 2, 2)),
            dma((2, 2, 4, 2)), dma((2, 2, 4, 2)),
            dma((2, 2, 3)), dma((2, 2, 3)),
            dma((8,)), dma((8,)),
            dma((4,)), dma((4,)),
            dma((2, 4)), dma((2, 4)),
            dma((2, 2, 4)), dma((2, 2, 4)),
            dma((2, 3, 4)), dma((2, 3, 4)),
            dma((2, 4)), dma((2, 4)),
        ],
        compiler_params=pltpu.CompilerParams(
            collective_id=0, has_side_effects=True, vmem_limit_bytes=56 * 2**20
        ),
        cost_estimate=pl.CostEstimate(flops=3758096384, bytes_accessed=20000000, transcendentals=1000000),
    )(activations, out_grads, clip_bound)


def solution(mesh):
    return jax.shard_map(
        body,
        mesh=mesh,
        in_specs=(P("dp", "tp", None), P("dp", None, "tp"), P()),
        out_specs=P("dp", "tp"),
        check_vma=False,
    )
```

```python
import math

import jax
import jax.numpy as jnp
from jax import lax
from jax.experimental import pallas as pl
from jax.experimental.pallas import tpu as pltpu
from jax.sharding import PartitionSpec as P

MESH = pl.DeviceIdType.MESH
F32 = jnp.float32
NX, NY, NZL, NZH = 4, 8, 4, 2
HALF = 32
ROWS = 112
TILE = 512
POWER, SHIFT = 11, 120
OFFSET = (0, 1, 3, 2)
OWN, FROM_RIGHT, FROM_LEFT, FAR = 0, 1, 2, 3


def encode(value, bound):
    u = (value.reshape(-1, 8, 256) * (2.0 ** (SHIFT / POWER) / bound)[None]).reshape(value.shape)
    u2 = u * u
    u4 = u2 * u2
    return ((u4 * u4) * (u2 * u)).astype(jnp.bfloat16)


def decode(code, bound):
    code = code.astype(F32)
    size = jnp.exp2(jnp.log(jnp.maximum(jnp.abs(code), 2.0**-126)) * (1.0 / (POWER * math.log(2.0))))
    size = (size.reshape(-1, 8, 256) * (2.0 ** (-SHIFT / POWER) * bound)[None]).reshape(code.shape)
    return jnp.where(code < 0, -size, size)


def kernel(
    act, grads_in, clip, out,
    grads, buf, relay, gr, prod, sq, sq_in, top, bound, bound_in, line_bound, limit_out, limit_in, sout, sin, yout, yin, zout, zin,
    load_sem, grads_sem, x_s, x_r, f_s, f_r, z_s, z_r, d_s, d_r, n_s, n_r, b_s, b_r, v_s, v_r, t_s, t_r, s_s, s_r, y_s, y_r, w_s, w_r,
):
    dp, tp = lax.axis_index("dp"), lax.axis_index("tp")
    y, zl = lax.div(dp, 4), lax.rem(dp, 4)
    zh, x, c = lax.div(tp, 8), lax.rem(lax.div(tp, 2), 4), lax.rem(tp, 2)
    z = zh * 4 + zl

    def peer(dx=0, dy=0, dz=0, dc=0):
        nz = lax.rem(z + dz, 8)
        return (
            lax.rem(y + dy, 8) * 4 + lax.rem(nz, 4),
            lax.div(nz, 4) * 8 + lax.rem(x + dx, 4) * 2 + lax.rem(c + dc, 2),
        )

    def line(r, dy=0):
        return (lax.rem(y + dy, 8) * 4 + lax.rem(zl + r, 4), tp)

    tp_peers = [(i, peer(dx=(i // 2) % 4, dz=4 * (i // 8), dc=i % 2)) for i in range(15, 0, -1)]
    z_far = {0: peer(dz=2), 1: peer(dz=6)}
    x_next = {0: peer(dx=1), 1: peer(dx=3)}
    y_next = {0: peer(dy=1), 1: peer(dy=7)}
    other = peer(dc=1)

    def unit(e, far, pos, core, h):
        return buf.at[e, 16 * far + 4 * pos + 2 * core + h]

    def remote(src, dst, s, r, to):
        return pltpu.make_async_remote_copy(
            src_ref=src, dst_ref=dst, send_sem=s, recv_sem=r, device_id=to, device_id_type=MESH
        )

    started = []

    def settle(count):
        for copy in started[:count]:
            copy.wait_send()
        del started[:count]

    def start(copy):
        copy.start()
        started.append(copy)

    def whole(e, far, pos, core):
        return buf.at[e, pl.ds(16 * far + 4 * pos + 2 * core, 2)]

    def x_copy(e, far, d):
        return remote(
            whole(e, far, OWN, 0), whole(e, far, FROM_LEFT if d == 0 else FROM_RIGHT, 0),
            x_s.at[e, far, d], x_r.at[e, far, d], x_next[d],
        )

    def f_copy(e, far, d):
        return remote(
            unit(e, far, FROM_LEFT if d == 0 else FROM_RIGHT, 0, d), unit(e, far, FAR, 0, d),
            f_s.at[e, far, d], f_r.at[e, far, d], x_next[d],
        )

    def z_copy(e, d, leg):
        src = unit(e, 0, OWN, 0, d) if leg == 0 else relay.at[e, d]
        dst = relay.at[e, d] if leg == 0 else unit(e, 1, OWN, 0, d)
        return remote(src, dst, z_s.at[e, d, leg], z_r.at[e, d, leg], z_far[d])

    def d_copy(e, far, pos):
        return remote(
            whole(e, far, pos, 0), whole(e, far, pos, 1), d_s.at[e, far, pos], d_r.at[e, far, pos], other
        )

    loads = {
        (e, h): pltpu.make_async_copy(
            act.at[e, pl.ds(h * HALF, HALF)], unit(e, 0, OWN, 0, h), load_sem.at[e, h]
        )
        for e in range(2) for h in range(2)
    }
    for load in loads.values():
        load.start()
    grads_load = pltpu.make_async_copy(grads_in, grads, grads_sem)
    grads_load.start()

    barrier = pltpu.get_barrier_semaphore()
    greeted = [to for _, to in tp_peers] + list(z_far.values())
    greeted += [peer(dy=k) for k in range(1, 8)]
    greeted += [line(r, dy) for r in range(1, 4) for dy in (0, 1, 7)]
    for to in greeted:
        pl.semaphore_signal(barrier, inc=1, device_id=to, device_id_type=MESH)
    pl.semaphore_wait(barrier, len(greeted))

    for e in range(2):
        for h in range(2):
            loads[e, h].wait()
        if e == 0:
            start(z_copy(0, 0, 0))
            start(z_copy(0, 1, 0))
        for d in range(2):
            start(x_copy(e, 0, d))
        start(d_copy(e, 0, OWN))

    grads_load.wait()
    for e in range(2):
        for far in range(2):
            for pos in range(4):
                for core in range(2):
                    block = (
                        lax.rem(zh + far, 2) * 8 + lax.rem(x + OFFSET[pos], 4) * 2 + lax.rem(c + core, 2)
                    )
                    rows = pl.ds(pl.multiple_of(block * 64, 64), 64)
                    gr[e, 8 * far + 2 * pos + core] = grads[e, rows, :]

    def pass_relay(e):
        for d in range(2):
            z_copy(e, d, 0).wait_recv()
            start(z_copy(e, d, 1))

    def take_z(e):
        for d in range(2):
            z_copy(e, d, 1).wait_recv()
        for d in range(2):
            start(x_copy(e, 1, d))
        start(d_copy(e, 1, OWN))

    def take_x(e, far):
        for d in range(2):
            x_copy(e, far, d).wait_recv()
            start(f_copy(e, far, d))
            start(d_copy(e, far, FROM_LEFT if d == 0 else FROM_RIGHT))

    def take_far(e, far):
        for d in range(2):
            f_copy(e, far, d).wait_recv()
        start(d_copy(e, far, FAR))

    def wait_core(e, far, positions):
        for pos in positions:
            d_copy(e, far, pos).wait_recv()

    def multiply(e, lo, hi):
        first, last = lo == 0, hi == 8
        k = (hi - lo) * 128
        right = gr[e, 2 * lo:2 * hi].reshape(k, 256)

        def body(j, state):
            total, most = state
            cols = pl.ds(pl.multiple_of(j * TILE, TILE), TILE)
            left = buf[e, 4 * lo:4 * hi, :, cols].reshape(k, TILE)
            part = lax.dot_general(left, right, (((0,), (0,)), ((), ())), preferred_element_type=F32)
            if not first:
                part = part + prod[e, cols, :]
            prod[e, cols, :] = part
            if last:
                total = total + jnp.sum((part * part).reshape(TILE // 8, 8, 256), axis=0)
                most = jnp.maximum(most, jnp.max(jnp.abs(part).reshape(TILE // 8, 8, 256), axis=0))
            return total, most

        none = jnp.zeros((8, 256), F32)
        total, most = lax.fori_loop(0, 3584 // TILE, body, (none, none))
        if last:
            sq[e] = total
            top[e] = most
            for i, to in tp_peers:
                start(remote(sq.at[e], sq_in.at[e, i], n_s.at[e, i], n_r.at[e, i], to))

    def begins(d, r):
        return 4 if (r in (1, 3)) == (d == 0) else 3

    def block(e, row_y, r):
        rows = pl.ds(pl.multiple_of((row_y * 4 + lax.rem(zl + r, 4)) * ROWS, 16), ROWS)
        return prod[e, rows, :]

    def ahead(d, dist):
        return lax.rem(y + (dist if d == 0 else 8 - dist), 8)

    def tile_max(value):
        return jnp.broadcast_to(jnp.max(value, axis=(0, 1), keepdims=True), (8, 256))

    order = [(0, 1), (1, 2), (0, 3), (1, 0), (1, 1), (0, 2), (1, 3), (0, 0)]

    def s_copy(e, d, r):
        return remote(sout.at[e, d, r], sin.at[e, d, r], s_s.at[e, d, r], s_r.at[e, d, r], y_next[d])

    def w_copy(e, r):
        return remote(zout.at[e, r], zin.at[e, r], w_s.at[e, r], w_r.at[e, r], line(r))

    def first_hop(e):
        most = tile_max(top[e]) * 1.0001 + 1e-35
        for d, r in order:
            sout[e, d, r] = encode(block(e, ahead(d, begins(d, r)), r), most)
            start(s_copy(e, d, r))
        for r in range(1, 4):
            zout[e, r] = encode(block(e, y, r), most)
            start(w_copy(e, r))
        return most

    def factor(e):
        total = sq[e]
        for i, to in tp_peers:
            remote(sq.at[e], sq_in.at[e, i], n_s.at[e, i], n_r.at[e, i], to).wait_recv()
            total = total + sq_in[e, i]
        norm = jnp.sqrt(jnp.broadcast_to(jnp.sum(total, axis=(0, 1), keepdims=True), (8, 256)))
        return jnp.minimum(1.0, clip[0] / (norm + 1e-06))

    def b_copy(e, k):
        return remote(bound.at[e], bound_in.at[e, k], b_s.at[e, k], b_r.at[e, k], peer(dy=k))

    def send_bound(e, value):
        bound[e] = value
        for k in (1, 7, 2, 6, 3, 5, 4):
            start(b_copy(e, k))

    pass_relay(0)
    take_x(0, 0)
    take_x(1, 0)
    take_z(0)
    start(z_copy(1, 0, 0))
    start(z_copy(1, 1, 0))
    wait_core(0, 0, [OWN, FROM_RIGHT, FROM_LEFT])
    multiply(0, 0, 3)
    pass_relay(1)
    wait_core(1, 0, [OWN, FROM_RIGHT, FROM_LEFT])
    multiply(1, 0, 3)
    take_far(0, 0)
    take_far(1, 0)
    take_x(0, 1)
    take_z(1)
    wait_core(0, 0, [FAR])
    wait_core(0, 1, [OWN, FROM_RIGHT, FROM_LEFT])
    multiply(0, 3, 7)
    take_far(0, 1)
    wait_core(0, 1, [FAR])
    multiply(0, 7, 8)
    wait_core(1, 0, [FAR])
    wait_core(1, 1, [OWN])
    multiply(1, 3, 5)
    take_x(1, 1)
    most0 = first_hop(0)
    wait_core(1, 1, [FROM_RIGHT, FROM_LEFT])
    multiply(1, 5, 7)
    factor0 = factor(0)
    bound0 = factor0 * most0
    send_bound(0, bound0)
    take_far(1, 1)
    wait_core(1, 1, [FAR])
    multiply(1, 7, 8)
    most1 = first_hop(1)
    factor1 = factor(1)
    bound1 = factor1 * most1
    send_bound(1, bound1)
    mine = bound0 + bound1

    def own(row_y, r):
        terms = [
            scale[None] * block(e, row_y, r).reshape(ROWS // 8, 8, 256)
            for e, scale in enumerate((factor0, factor1))
        ]
        return (terms[0] + terms[1]).reshape(ROWS, 256)

    def v_copy(r):
        return remote(bound, line_bound.at[r], v_s.at[r], v_r.at[r], line(r))

    for r in range(1, 4):
        start(v_copy(r))

    def t_copy(d, r):
        return remote(
            limit_out.at[d, begins(d, r) - 3], limit_in.at[d, r], t_s.at[d, r], t_r.at[d, r],
            line(r, 1 if d == 0 else 7),
        )

    def y_copy(d, dist, r):
        return remote(
            yout.at[d, dist - 1, r], yin.at[d, dist - 1, r],
            y_s.at[d, dist - 1, r], y_r.at[d, dist - 1, r],
            y_next[d] if dist > 1 else line(r, 1 if d == 0 else 7),
        )

    bounds, sums = {}, {}

    def near(k):
        if k not in bounds:
            for e in range(2):
                b_copy(e, k).wait_recv()
            bounds[k] = bound_in[0, k] + bound_in[1, k]
        return bounds[k]

    def near_sum(d, n):
        if (d, n) not in sums:
            value = near(n if d == 0 else 8 - n)
            sums[d, n] = value if n == 1 else near_sum(d, n - 1) + value
        return sums[d, n]

    def arrived(d, dist, r):
        steps = begins(d, r) - dist
        if steps > 1:
            y_copy(d, dist + 1, r).wait_recv()
            return decode(yin[d, dist, r], near_sum(d, steps))
        value = 0.0
        for e in range(2):
            s_copy(e, d, r).wait_recv()
            value = value + decode(sin[e, d, r], bound_in[e, 1 if d == 0 else 7])
        return value

    def pass_on(steps, d, r):
        dist = begins(d, r) - steps
        limit = mine + near_sum(d, steps)
        value = own(ahead(d, dist), r) + arrived(d, dist, r)
        yout[d, dist - 1, r] = encode(value, limit)
        start(y_copy(d, dist, r))

    for d, r in order:
        pass_on(1, d, r)
    for d in range(2):
        for k in range(2):
            limit_out[d, k] = mine + near_sum(d, k + 2)
    for r in range(1, 4):
        for d in range(2):
            start(t_copy(d, r))
    for steps in (2, 3):
        for d, r in order:
            if begins(d, r) > steps:
                pass_on(steps, d, r)

    result = own(y, 0)
    for r in range(1, 4):
        v_copy(r).wait_recv()
        for e in range(2):
            w_copy(e, r).wait_recv()
            result = result + decode(zin[e, r], line_bound[r, e])
    settle(len(started) - 12)
    for d, r in order[4:] + order[:4]:
        if r == 0:
            result = result + arrived(d, 0, 0)
        else:
            t_copy(d, r).wait_recv()
            y_copy(d, 1, r).wait_recv()
            result = result + decode(yin[d, 0, r], limit_in[d, r])
    out[...] = result
    settle(len(started))


def body(activations, out_grads, clip_bound):
    vmem, dma = pltpu.VMEM, pltpu.SemaphoreType.DMA
    return pl.pallas_call(
        kernel,
        out_shape=jax.ShapeDtypeStruct((ROWS, 256), F32),
        in_specs=[
            pl.BlockSpec(memory_space=pl.ANY),
            pl.BlockSpec(memory_space=pl.ANY),
            pl.BlockSpec(memory_space=pltpu.SMEM),
        ],
        out_specs=pl.BlockSpec(memory_space=pltpu.VMEM),
        scratch_shapes=[
            vmem((2, 1024, 256), jnp.bfloat16),
            vmem((2, 32, HALF, 3584), jnp.bfloat16),
            vmem((2, 2, HALF, 3584), jnp.bfloat16),
            vmem((2, 16, 64, 256), jnp.bfloat16),
            vmem((2, 3584, 256), F32),
            vmem((2, 8, 256), F32),
            vmem((2, 16, 8, 256), F32),
            vmem((2, 8, 256), F32),
            vmem((2, 8, 256), F32),
            vmem((2, 8, 8, 256), F32),
            vmem((4, 2, 8, 256), F32),
            vmem((2, 2, 8, 256), F32),
            vmem((2, 4, 8, 256), F32),
            vmem((2, 2, 4, ROWS, 256), jnp.bfloat16),
            vmem((2, 2, 4, ROWS, 256), jnp.bfloat16),
            vmem((2, 3, 4, ROWS, 256), jnp.bfloat16),
            vmem((2, 3, 4, ROWS, 256), jnp.bfloat16),
            vmem((2, 4, ROWS, 256), jnp.bfloat16),
            vmem((2, 4, ROWS, 256), jnp.bfloat16),
            dma((2, 2)),
            dma,
            dma((2, 2, 2)), dma((2, 2, 2)),
            dma((2, 2, 2)), dma((2, 2, 2)),
            dma((2, 2, 2)), dma((2, 2, 2)),
            dma((2, 2, 4)), dma((2, 2, 4)),
            dma((2, 16)), dma((2, 16)),
            dma((2, 8)), dma((2, 8)),
            dma((4,)), dma((4,)),
            dma((2, 4)), dma((2, 4)),
            dma((2, 2, 4)), dma((2, 2, 4)),
            dma((2, 3, 4)), dma((2, 3, 4)),
            dma((2, 4)), dma((2, 4)),
        ],
        compiler_params=pltpu.CompilerParams(
            collective_id=0, has_side_effects=True, vmem_limit_bytes=56 * 2**20
        ),
        cost_estimate=pl.CostEstimate(flops=3758096384, bytes_accessed=20000000, transcendentals=1000000),
    )(activations, out_grads, clip_bound)


def solution(mesh):
    return jax.shard_map(
        body,
        mesh=mesh,
        in_specs=(P("dp", "tp", None), P("dp", None, "tp"), P()),
        out_specs=P("dp", "tp"),
        check_vma=False,
    )
```

```python
import math

import jax
import jax.numpy as jnp
from jax import lax
from jax.experimental import pallas as pl
from jax.experimental.pallas import tpu as pltpu
from jax.sharding import PartitionSpec as P

MESH = pl.DeviceIdType.MESH
F32 = jnp.float32
NX, NY, NZL, NZH = 4, 8, 4, 2
HALF = 32
ROWS = 112
TILE = 512
POWER, SHIFT = 11, 120
OFFSET = (0, 1, 3, 2)
OWN, FROM_RIGHT, FROM_LEFT, FAR = 0, 1, 2, 3


def encode(value, bound):
    u = (value.reshape(-1, 8, 256) * (2.0 ** (SHIFT / POWER) / bound)[None]).reshape(value.shape)
    u2 = u * u
    u4 = u2 * u2
    return ((u4 * u4) * (u2 * u)).astype(jnp.bfloat16)


def decode(code, bound):
    code = code.astype(F32)
    size = jnp.exp2(jnp.log(jnp.maximum(jnp.abs(code), 2.0**-126)) * (1.0 / (POWER * math.log(2.0))))
    size = (size.reshape(-1, 8, 256) * (2.0 ** (-SHIFT / POWER) * bound)[None]).reshape(code.shape)
    return jnp.where(code < 0, -size, size)


def kernel(
    act, grads_in, clip, out,
    grads, buf, relay, gr, prod, sq, sq_in, top, bound, bound_in, line_bound, limit_out, limit_in, sout, sin, yout, yin, zout, zin,
    load_sem, grads_sem, x_s, x_r, f_s, f_r, z_s, z_r, d_s, d_r, n_s, n_r, b_s, b_r, v_s, v_r, t_s, t_r, s_s, s_r, y_s, y_r, w_s, w_r,
):
    dp, tp = lax.axis_index("dp"), lax.axis_index("tp")
    y, zl = lax.div(dp, 4), lax.rem(dp, 4)
    zh, x, c = lax.div(tp, 8), lax.rem(lax.div(tp, 2), 4), lax.rem(tp, 2)
    z = zh * 4 + zl

    def peer(dx=0, dy=0, dz=0, dc=0):
        nz = lax.rem(z + dz, 8)
        return (
            lax.rem(y + dy, 8) * 4 + lax.rem(nz, 4),
            lax.div(nz, 4) * 8 + lax.rem(x + dx, 4) * 2 + lax.rem(c + dc, 2),
        )

    def line(r, dy=0):
        return (lax.rem(y + dy, 8) * 4 + lax.rem(zl + r, 4), tp)

    tp_peers = [(i, peer(dx=(i // 2) % 4, dz=4 * (i // 8), dc=i % 2)) for i in range(15, 0, -1)]
    z_far = {0: peer(dz=2), 1: peer(dz=6)}
    x_next = {0: peer(dx=1), 1: peer(dx=3)}
    y_next = {0: peer(dy=1), 1: peer(dy=7)}
    other = peer(dc=1)

    def unit(e, far, pos, core, h):
        return buf.at[e, 16 * far + 4 * pos + 2 * core + h]

    def remote(src, dst, s, r, to):
        return pltpu.make_async_remote_copy(
            src_ref=src, dst_ref=dst, send_sem=s, recv_sem=r, device_id=to, device_id_type=MESH
        )

    started = []

    def settle(count):
        for copy in started[:count]:
            copy.wait_send()
        del started[:count]

    def start(copy):
        copy.start()
        started.append(copy)

    def x_copy(e, far, d, h):
        return remote(
            unit(e, far, OWN, 0, h), unit(e, far, FROM_LEFT if d == 0 else FROM_RIGHT, 0, h),
            x_s.at[e, far, d, h], x_r.at[e, far, d, h], x_next[d],
        )

    def f_copy(e, far, d):
        return remote(
            unit(e, far, FROM_LEFT if d == 0 else FROM_RIGHT, 0, d), unit(e, far, FAR, 0, d),
            f_s.at[e, far, d], f_r.at[e, far, d], x_next[d],
        )

    def z_copy(e, d, leg):
        src = unit(e, 0, OWN, 0, d) if leg == 0 else relay.at[e, d]
        dst = relay.at[e, d] if leg == 0 else unit(e, 1, OWN, 0, d)
        return remote(src, dst, z_s.at[e, d, leg], z_r.at[e, d, leg], z_far[d])

    def d_copy(e, far, pos, h):
        return remote(
            unit(e, far, pos, 0, h), unit(e, far, pos, 1, h),
            d_s.at[e, far, pos, h], d_r.at[e, far, pos, h], other,
        )

    loads = {
        (e, h): pltpu.make_async_copy(
            act.at[e, pl.ds(h * HALF, HALF)], unit(e, 0, OWN, 0, h), load_sem.at[e, h]
        )
        for e in range(2) for h in range(2)
    }
    for load in loads.values():
        load.start()
    grads_load = pltpu.make_async_copy(grads_in, grads, grads_sem)
    grads_load.start()

    barrier = pltpu.get_barrier_semaphore()
    greeted = [to for _, to in tp_peers] + list(z_far.values())
    greeted += [peer(dy=k) for k in range(1, 8)]
    greeted += [line(r, dy) for r in range(1, 4) for dy in (0, 1, 7)]
    for to in greeted:
        pl.semaphore_signal(barrier, inc=1, device_id=to, device_id_type=MESH)
    pl.semaphore_wait(barrier, len(greeted))

    for e in range(2):
        for h in range(2):
            loads[e, h].wait()
        if e == 0:
            start(z_copy(0, 0, 0))
            start(z_copy(0, 1, 0))
        for h in range(2):
            for d in range(2):
                start(x_copy(e, 0, d, h if d == 0 else 1 - h))
        for h in range(2):
            start(d_copy(e, 0, OWN, h))

    grads_load.wait()
    for e in range(2):
        for far in range(2):
            for pos in range(4):
                for core in range(2):
                    block = (
                        lax.rem(zh + far, 2) * 8 + lax.rem(x + OFFSET[pos], 4) * 2 + lax.rem(c + core, 2)
                    )
                    rows = pl.ds(pl.multiple_of(block * 64, 64), 64)
                    gr[e, 8 * far + 2 * pos + core] = grads[e, rows, :]

    def pass_relay(e):
        for d in range(2):
            z_copy(e, d, 0).wait_recv()
            start(z_copy(e, d, 1))

    def take_z(e):
        for d in range(2):
            z_copy(e, d, 1).wait_recv()
            for k in range(2):
                start(x_copy(e, 1, k, d))
            start(d_copy(e, 1, OWN, d))

    def take_x(e, far):
        for step in range(2):
            for d in range(2):
                h = d if step == 0 else 1 - d
                x_copy(e, far, d, h).wait_recv()
                if step == 0:
                    start(f_copy(e, far, d))
                start(d_copy(e, far, FROM_LEFT if d == 0 else FROM_RIGHT, h))

    def take_far(e, far):
        for d in range(2):
            f_copy(e, far, d).wait_recv()
            start(d_copy(e, far, FAR, d))

    def wait_core(e, far, positions):
        for pos in positions:
            for h in range(2):
                d_copy(e, far, pos, h).wait_recv()

    def multiply(e, lo, hi):
        first, last = lo == 0, hi == 8
        k = (hi - lo) * 128
        right = gr[e, 2 * lo:2 * hi].reshape(k, 256)

        def body(j, state):
            total, most = state
            cols = pl.ds(pl.multiple_of(j * TILE, TILE), TILE)
            left = buf[e, 4 * lo:4 * hi, :, cols].reshape(k, TILE)
            part = lax.dot_general(left, right, (((0,), (0,)), ((), ())), preferred_element_type=F32)
            if not first:
                part = part + prod[e, cols, :]
            prod[e, cols, :] = part
            if last:
                total = total + jnp.sum((part * part).reshape(TILE // 8, 8, 256), axis=0)
                most = jnp.maximum(most, jnp.max(jnp.abs(part).reshape(TILE // 8, 8, 256), axis=0))
            return total, most

        none = jnp.zeros((8, 256), F32)
        total, most = lax.fori_loop(0, 3584 // TILE, body, (none, none))
        if last:
            sq[e] = total
            top[e] = most
            for i, to in tp_peers:
                start(remote(sq.at[e], sq_in.at[e, i], n_s.at[e, i], n_r.at[e, i], to))

    def begins(d, r):
        return 4 if (r in (1, 3)) == (d == 0) else 3

    def block(e, row_y, r):
        rows = pl.ds(pl.multiple_of((row_y * 4 + lax.rem(zl + r, 4)) * ROWS, 16), ROWS)
        return prod[e, rows, :]

    def ahead(d, dist):
        return lax.rem(y + (dist if d == 0 else 8 - dist), 8)

    def tile_max(value):
        return jnp.broadcast_to(jnp.max(value, axis=(0, 1), keepdims=True), (8, 256))

    order = [(0, 1), (1, 2), (0, 3), (1, 0), (1, 1), (0, 2), (1, 3), (0, 0)]

    def s_copy(e, d, r):
        return remote(sout.at[e, d, r], sin.at[e, d, r], s_s.at[e, d, r], s_r.at[e, d, r], y_next[d])

    def w_copy(e, r):
        return remote(zout.at[e, r], zin.at[e, r], w_s.at[e, r], w_r.at[e, r], line(r))

    def first_hop(e):
        most = tile_max(top[e]) * 1.0001 + 1e-35
        for d, r in order:
            sout[e, d, r] = encode(block(e, ahead(d, begins(d, r)), r), most)
            start(s_copy(e, d, r))
        for r in range(1, 4):
            zout[e, r] = encode(block(e, y, r), most)
            start(w_copy(e, r))
        return most

    def factor(e):
        total = sq[e]
        for i, to in tp_peers:
            remote(sq.at[e], sq_in.at[e, i], n_s.at[e, i], n_r.at[e, i], to).wait_recv()
            total = total + sq_in[e, i]
        norm = jnp.sqrt(jnp.broadcast_to(jnp.sum(total, axis=(0, 1), keepdims=True), (8, 256)))
        return jnp.minimum(1.0, clip[0] / (norm + 1e-06))

    def b_copy(e, k):
        return remote(bound.at[e], bound_in.at[e, k], b_s.at[e, k], b_r.at[e, k], peer(dy=k))

    def send_bound(e, value):
        bound[e] = value
        for k in (1, 7, 2, 6, 3, 5, 4):
            start(b_copy(e, k))

    pass_relay(0)
    take_x(0, 0)
    take_x(1, 0)
    take_z(0)
    start(z_copy(1, 0, 0))
    start(z_copy(1, 1, 0))
    for e in range(2):
        wait_core(e, 0, [OWN, FROM_RIGHT, FROM_LEFT])
        multiply(e, 0, 3)
    pass_relay(1)
    take_far(0, 0)
    take_far(1, 0)
    take_x(0, 1)
    take_z(1)
    wait_core(0, 0, [FAR])
    wait_core(0, 1, [OWN, FROM_RIGHT, FROM_LEFT])
    multiply(0, 3, 7)
    take_far(0, 1)
    wait_core(0, 1, [FAR])
    multiply(0, 7, 8)
    take_x(1, 1)
    most0 = first_hop(0)
    wait_core(1, 0, [FAR])
    wait_core(1, 1, [OWN, FROM_RIGHT, FROM_LEFT])
    multiply(1, 3, 7)
    factor0 = factor(0)
    bound0 = factor0 * most0
    send_bound(0, bound0)
    take_far(1, 1)
    wait_core(1, 1, [FAR])
    multiply(1, 7, 8)
    most1 = first_hop(1)
    factor1 = factor(1)
    bound1 = factor1 * most1
    send_bound(1, bound1)
    mine = bound0 + bound1

    def own(row_y, r):
        terms = [
            scale[None] * block(e, row_y, r).reshape(ROWS // 8, 8, 256)
            for e, scale in enumerate((factor0, factor1))
        ]
        return (terms[0] + terms[1]).reshape(ROWS, 256)

    def v_copy(r):
        return remote(bound, line_bound.at[r], v_s.at[r], v_r.at[r], line(r))

    for r in range(1, 4):
        start(v_copy(r))

    def t_copy(d, r):
        return remote(
            limit_out.at[d, begins(d, r) - 3], limit_in.at[d, r], t_s.at[d, r], t_r.at[d, r],
            line(r, 1 if d == 0 else 7),
        )

    def y_copy(d, dist, r):
        return remote(
            yout.at[d, dist - 1, r], yin.at[d, dist - 1, r],
            y_s.at[d, dist - 1, r], y_r.at[d, dist - 1, r],
            y_next[d] if dist > 1 else line(r, 1 if d == 0 else 7),
        )

    bounds, sums = {}, {}

    def near(k):
        if k not in bounds:
            for e in range(2):
                b_copy(e, k).wait_recv()
            bounds[k] = bound_in[0, k] + bound_in[1, k]
        return bounds[k]

    def near_sum(d, n):
        if (d, n) not in sums:
            value = near(n if d == 0 else 8 - n)
            sums[d, n] = value if n == 1 else near_sum(d, n - 1) + value
        return sums[d, n]

    def arrived(d, dist, r):
        steps = begins(d, r) - dist
        if steps > 1:
            y_copy(d, dist + 1, r).wait_recv()
            return decode(yin[d, dist, r], near_sum(d, steps))
        value = 0.0
        for e in range(2):
            s_copy(e, d, r).wait_recv()
            value = value + decode(sin[e, d, r], bound_in[e, 1 if d == 0 else 7])
        return value

    def pass_on(steps, d, r):
        dist = begins(d, r) - steps
        limit = mine + near_sum(d, steps)
        value = own(ahead(d, dist), r) + arrived(d, dist, r)
        yout[d, dist - 1, r] = encode(value, limit)
        start(y_copy(d, dist, r))

    for d, r in order:
        pass_on(1, d, r)
    for d in range(2):
        for k in range(2):
            limit_out[d, k] = mine + near_sum(d, k + 2)
    for r in range(1, 4):
        for d in range(2):
            start(t_copy(d, r))
    for steps in (2, 3):
        for d, r in order:
            if begins(d, r) > steps:
                pass_on(steps, d, r)

    result = own(y, 0)
    for r in range(1, 4):
        v_copy(r).wait_recv()
        for e in range(2):
            w_copy(e, r).wait_recv()
            result = result + decode(zin[e, r], line_bound[r, e])
    settle(len(started) - 12)
    for d, r in order[4:] + order[:4]:
        if r == 0:
            result = result + arrived(d, 0, 0)
        else:
            t_copy(d, r).wait_recv()
            y_copy(d, 1, r).wait_recv()
            result = result + decode(yin[d, 0, r], limit_in[d, r])
    out[...] = result
    settle(len(started))


def body(activations, out_grads, clip_bound):
    vmem, dma = pltpu.VMEM, pltpu.SemaphoreType.DMA
    return pl.pallas_call(
        kernel,
        out_shape=jax.ShapeDtypeStruct((ROWS, 256), F32),
        in_specs=[
            pl.BlockSpec(memory_space=pl.ANY),
            pl.BlockSpec(memory_space=pl.ANY),
            pl.BlockSpec(memory_space=pltpu.SMEM),
        ],
        out_specs=pl.BlockSpec(memory_space=pltpu.VMEM),
        scratch_shapes=[
            vmem((2, 1024, 256), jnp.bfloat16),
            vmem((2, 32, HALF, 3584), jnp.bfloat16),
            vmem((2, 2, HALF, 3584), jnp.bfloat16),
            vmem((2, 16, 64, 256), jnp.bfloat16),
            vmem((2, 3584, 256), F32),
            vmem((2, 8, 256), F32),
            vmem((2, 16, 8, 256), F32),
            vmem((2, 8, 256), F32),
            vmem((2, 8, 256), F32),
            vmem((2, 8, 8, 256), F32),
            vmem((4, 2, 8, 256), F32),
            vmem((2, 2, 8, 256), F32),
            vmem((2, 4, 8, 256), F32),
            vmem((2, 2, 4, ROWS, 256), jnp.bfloat16),
            vmem((2, 2, 4, ROWS, 256), jnp.bfloat16),
            vmem((2, 3, 4, ROWS, 256), jnp.bfloat16),
            vmem((2, 3, 4, ROWS, 256), jnp.bfloat16),
            vmem((2, 4, ROWS, 256), jnp.bfloat16),
            vmem((2, 4, ROWS, 256), jnp.bfloat16),
            dma((2, 2)),
            dma,
            dma((2, 2, 2, 2)), dma((2, 2, 2, 2)),
            dma((2, 2, 2)), dma((2, 2, 2)),
            dma((2, 2, 2)), dma((2, 2, 2)),
            dma((2, 2, 4, 2)), dma((2, 2, 4, 2)),
            dma((2, 16)), dma((2, 16)),
            dma((2, 8)), dma((2, 8)),
            dma((4,)), dma((4,)),
            dma((2, 4)), dma((2, 4)),
            dma((2, 2, 4)), dma((2, 2, 4)),
            dma((2, 3, 4)), dma((2, 3, 4)),
            dma((2, 4)), dma((2, 4)),
        ],
        compiler_params=pltpu.CompilerParams(
            collective_id=0, has_side_effects=True, vmem_limit_bytes=56 * 2**20
        ),
        cost_estimate=pl.CostEstimate(flops=3758096384, bytes_accessed=20000000, transcendentals=1000000),
    )(activations, out_grads, clip_bound)


def solution(mesh):
    return jax.shard_map(
        body,
        mesh=mesh,
        in_specs=(P("dp", "tp", None), P("dp", None, "tp"), P()),
        out_specs=P("dp", "tp"),
        check_vma=False,
    )
```
